256 devices in a mesh: row: 32 (over y, z), col: 4 (over x), rep: 2 (over core).
Axes of the slice: x: 4, y: 4, z: 8, core: 2. Of those that a mesh axis runs over, the one named last changes fastest.
Arguments:
- tiles: float32 [32, 4, 32, 128, 128], P('row', 'col'), may hold values from -6 to 6
- block_row: int32 [32, 4, 32], P('row', 'col'), may hold values from 0 to 23
- block_col: int32 [32, 4, 32], P('row', 'col'), may hold values from 0 to 39
- live_rows: int32 [32, 4, 32], P('row', 'col'), may hold values from 0 to 128
- omega: float32 [4, 5120, 256], P('col', 'row', 'rep'), may hold values from -6 to 6
Outputs:
- basis: float32 [32, 3072, 256], P('row', 'col', 'rep')
- panel_basis: float32 [4, 5120, 256], P('col', 'row', 'rep')
The draws below stay inside these ranges and needn't reach their ends.
Inputs may be any that keep to these rules, and one draw needn't show every extreme that they name: A slot with live_rows 0 holds nothing; slots may repeat a block, and then add.
All inputs are finite; a program needn't handle non-finite values.
Results may differ from the reference program's by a relative error of at most 0.0003.
Values sent between devices are 32-bit elements; how exact they have to be, the bound alone decides.
No kernel may reach another device: no remote copies, remote signals or barrier semaphores. Data moves between devices by JAX's collectives and lax.ppermute only.
A program may use at most 128 MiB of HBM per device.

```python
import math
import jax
import jax.numpy as jnp
import numpy as np
from jax import lax

BS = 128
K = 256
ITERS = 2
RB_DEV = 24
CB_DEV = 40
NB = 32
GRID_ROWS = 32
GRID_COLS = 4
ROWS_GRP = 3072
COLS_GRP = 5120
NROWS = 98304
NCOLS = 20480


def set_ends(array, stream_key, low, high):
    longest = array.shape.index(max(array.shape))
    spots = []
    for shift in (0, 1):
        where = [jax.random.randint(jax.random.fold_in(stream_key, axis), (), 0, length) for axis, length in enumerate(array.shape)]
        where[longest] = (where[longest] + shift) % array.shape[longest]
        spots.append(tuple(where))
    return array.at[spots[0]].set(low).at[spots[1]].set(high)


def block_levels(own_key, extent, cuts, least, high):
    level = 1.0
    for position, shards_of in cuts:
        heights = jax.random.uniform(jax.random.fold_in(jax.random.fold_in(own_key, 6), position), (shards_of,), jnp.float32, least / len(cuts), high / len(cuts))
        level = level * jnp.repeat(jnp.exp(heights), extent[position] // shards_of).reshape((-1,) + (1,) * (len(extent) - 1 - position))
    return level


def rank_table(number_of, lean):
    portions = [(1 << 20) // math.isqrt(standing ** lean) + 1 for standing in range(1, number_of + 1)]
    width = 1 + sum(portions) // (1 << 30)
    return np.cumsum(np.array([max(1, weight // width) for weight in portions]))


def ranked_ids(key, extent, count, lean):
    listing = rank_table(count, lean)
    lot = jax.random.randint(jax.random.fold_in(key, 1), extent, 0, int(listing[count - 1]))
    standing = jnp.searchsorted(jnp.asarray(listing, jnp.int32), lot, side="right")
    return jax.random.permutation(jax.random.fold_in(key, 2), count)[standing].astype(jnp.int32)


def normal_values(key, shape, spread, bound, cuts=(), kind=jnp.bfloat16):
    loudness = block_levels(key, shape, cuts, -0.22, 0.18) if cuts else 1.0
    values = jax.random.normal(key, shape, jnp.float32) * spread * loudness
    return jnp.minimum(jnp.maximum(values, -bound), bound).astype(kind)


def setup_inputs(seed: int = 0) -> dict:
    arg_keys = jax.random.split(jax.random.key(seed), 6)
    tiles = normal_values(arg_keys[0], (GRID_ROWS, GRID_COLS, NB, BS, BS), 1.0, 6.0, ((0, 32), (1, 4)), jnp.float32)
    block_row = set_ends(ranked_ids(arg_keys[1], (GRID_ROWS, GRID_COLS, NB), RB_DEV, 1), jax.random.fold_in(arg_keys[1], 3), 0, RB_DEV - 1).astype(jnp.int32)
    block_col = set_ends(ranked_ids(arg_keys[2], (GRID_ROWS, GRID_COLS, NB), CB_DEV, 1), jax.random.fold_in(arg_keys[2], 3), 0, CB_DEV - 1).astype(jnp.int32)
    live_rows = set_ends(jax.random.randint(arg_keys[3], (GRID_ROWS, GRID_COLS, NB), 0, BS + 1), jax.random.fold_in(arg_keys[3], 1), 0, BS).astype(jnp.int32)
    omega = normal_values(arg_keys[4], (GRID_COLS, COLS_GRP, K), 1.0, 6.0, ((0, 4), (1, 32), (2, 2)), jnp.float32)
    return dict(tiles=tiles, block_row=block_row, block_col=block_col, live_rows=live_rows, omega=omega)


def masked_tiles(tiles, live_rows):
    rows = lax.broadcasted_iota(jnp.int32, tiles.shape, tiles.ndim - 2)
    return jnp.where(rows < live_rows.astype(jnp.int32)[..., None, None], tiles, jnp.float32(0.0))

def forward(masked, block_row, block_col, panel):
    blocked = panel.reshape(GRID_COLS * CB_DEV, BS, K)
    offsets = (jnp.arange(GRID_COLS, dtype=jnp.int32) * CB_DEV)[:, None]

    def one_row(pieces):
        tiles_r, rows_r, cols_r = pieces
        picked = blocked[(cols_r.astype(jnp.int32) + offsets).reshape(-1)]
        flat_tiles = tiles_r.reshape(GRID_COLS * NB, BS, BS)
        product = jnp.einsum('sab,sbk->sak', flat_tiles, picked, precision=lax.Precision.HIGHEST)
        summed = jax.ops.segment_sum(product, rows_r.reshape(-1), num_segments=RB_DEV)
        return summed.reshape(ROWS_GRP, K)
    return lax.map(one_row, (masked, block_row, block_col))

def backward(masked, block_row, block_col, basis_rows):
    blocked = basis_rows.reshape(GRID_ROWS, RB_DEV, BS, K)
    offsets = (jnp.arange(GRID_COLS, dtype=jnp.int32) * CB_DEV)[:, None]

    def step(total, pieces):
        tiles_r, rows_r, cols_r, basis_r = pieces
        picked = basis_r[rows_r.reshape(-1)]
        flat_tiles = tiles_r.reshape(GRID_COLS * NB, BS, BS)
        product = jnp.einsum('sab,sak->sbk', flat_tiles, picked, precision=lax.Precision.HIGHEST)
        target = (cols_r.astype(jnp.int32) + offsets).reshape(-1)
        return (total + jax.ops.segment_sum(product, target, num_segments=GRID_COLS * CB_DEV), None)
    start = jnp.zeros((GRID_COLS * CB_DEV, BS, K), jnp.float32)
    total, unused = lax.scan(step, start, (masked, block_row, block_col, blocked))
    return total.reshape(GRID_COLS, COLS_GRP, K)

def orthonormal(matrix):
    gram = jnp.dot(matrix.T.astype(jnp.float32), matrix.astype(jnp.float32), precision=lax.Precision.HIGHEST, preferred_element_type=jnp.float32)
    lower = jnp.linalg.cholesky(gram)
    return jax.scipy.linalg.solve_triangular(lower, matrix.T, lower=True).T

def reference(tiles, block_row, block_col, live_rows, omega):
    masked = masked_tiles(tiles, live_rows)
    sketch = forward(masked, block_row, block_col, omega)
    basis_rows = orthonormal(sketch.reshape(NROWS, K)).reshape(GRID_ROWS, ROWS_GRP, K)
    panel = omega
    for step in range(ITERS):
        other = backward(masked, block_row, block_col, basis_rows)
        panel = orthonormal(other.reshape(GRID_COLS * COLS_GRP, K)).reshape(GRID_COLS, COLS_GRP, K)
        sketch = forward(masked, block_row, block_col, panel)
        basis_rows = orthonormal(sketch.reshape(NROWS, K)).reshape(GRID_ROWS, ROWS_GRP, K)
    return (basis_rows * math.sqrt(NROWS), panel * math.sqrt(NCOLS))
```

```python
import math

import jax
import jax.numpy as jnp
from jax import lax
from jax.experimental import pallas as pl
from jax.experimental.pallas import tpu as pltpu
from jax.sharding import Mesh
from jax.sharding import PartitionSpec as P

ITERS = 2
RB_DEV = 24
CB_DEV = 40
BS = 128
HALF = 128
NY = 4
NZ = 8
NX = 4
ROWS_OWN = 768
COLS_OWN = 160
UNROLL = 4
F32 = jnp.float32
BF16 = jnp.bfloat16
VMEM_LIMIT = 40 * 1024 * 1024


def dot_nn(a, b):
    return lax.dot_general(
        a, b, (((1,), (0,)), ((), ())), precision=lax.Precision.HIGHEST, preferred_element_type=F32
    )


def dot_nt(a, b):
    return lax.dot_general(
        a, b, (((1,), (1,)), ((), ())), precision=lax.Precision.HIGHEST, preferred_element_type=F32
    )


def dot_tn(a, b):
    return lax.dot_general(
        a, b, (((0,), (0,)), ((), ())), precision=lax.Precision.HIGHEST, preferred_element_type=F32
    )


def split(x):
    high = x.astype(BF16)
    return high, (x - high.astype(F32)).astype(BF16)


def product_of(tile, block, dims):
    tile_high, tile_low = split(tile)
    high, low = split(block)

    def mul(a, b):
        return lax.dot_general(a, b, (dims, ((), ())), preferred_element_type=F32)

    return mul(tile_high, high) + (mul(tile_high, low) + mul(tile_low, high))


def masked_tile(tiles_ref, live_ref, slot):
    iota = lax.broadcasted_iota(jnp.int32, (BS, BS), 0)
    return jnp.where(iota < live_ref[slot], tiles_ref[slot], F32(0.0))


def block_at(index):
    return pl.ds(pl.multiple_of(index * BS, BS), BS)


def accumulate(slots, held, total, from_ref, to_ref, shift, count, tiles_ref, live_ref, dims):
    def body(step, carry):
        base = step * UNROLL
        products = []
        for offset in range(UNROLL):
            slot = base + offset
            tile = masked_tile(tiles_ref, live_ref, slot)
            products.append(product_of(tile, held[block_at(from_ref[slot]), :], dims))
        for offset in range(UNROLL):
            place = lax.rem(to_ref[base + offset] + (count - shift), count)
            total[block_at(place), :] += products[offset]
        return carry

    total[...] = jnp.zeros_like(total)
    lax.fori_loop(0, slots // UNROLL, body, 0)


def forward_kernel(pos, rows, cols, live, tiles, p0, p1, p2, p3, o0, o1, o2, o3, held, total):
    y, z, x = pos[0], pos[1], pos[2]
    for j, piece in enumerate((p0, p1, p2, p3)):
        from_y = lax.rem(y + (NY - j), NY)
        for k in range(NZ):
            from_z = lax.rem(z + (NZ - k), NZ)
            place = pl.multiple_of((from_y * NZ + from_z) * COLS_OWN, 32)
            held[pl.ds(place, COLS_OWN), :] = piece[k * COLS_OWN : (k + 1) * COLS_OWN, :]
    accumulate(
        tiles.shape[0], held, total, cols, rows, x * (RB_DEV // NX), RB_DEV, tiles, live, ((1,), (0,))
    )
    for k, out in enumerate((o0, o1, o2, o3)):
        out[...] = total[k * ROWS_OWN : (k + 1) * ROWS_OWN, :]


def backward_kernel(pos, rows, cols, live, tiles, p0, p1, p2, p3, o0, o1, o2, o3, held, total):
    y, x = pos[0], pos[2]
    for j, piece in enumerate((p0, p1, p2, p3)):
        from_x = lax.rem(x + (NX - j), NX)
        held[pl.ds(pl.multiple_of(from_x * ROWS_OWN, 256), ROWS_OWN), :] = piece[...]
    accumulate(
        tiles.shape[0], held, total, rows, cols, y * (CB_DEV // NY), CB_DEV, tiles, live, ((0,), (0,))
    )
    size = CB_DEV // NY * BS
    for k, out in enumerate((o0, o1, o2, o3)):
        out[...] = total[k * size : (k + 1) * size, :]


def sum_kernel(*refs):
    out = refs[-1]
    value = refs[0][...]
    for ref in refs[1:-1]:
        value = value + ref[...]
    out[...] = value


def sum_split_kernel(pos, p0, p1, p2, p3, *outs):
    z = pos[1]
    for k, out in enumerate(outs):
        place = pl.ds(pl.multiple_of(lax.rem(z + k, NZ) * COLS_OWN, 32), COLS_OWN)
        out[...] = (p0[place, :] + p1[place, :]) + (p2[place, :] + p3[place, :])


def halves(pos, own, other):
    first = pos[3] == 0
    a, b = own[...], other[...]
    return jnp.where(first, a, b), jnp.where(first, b, a)


def gram_kernel(pos, own, other, gram):
    left, right = halves(pos, own, other)
    mine = own[...]
    gram[0:HALF, :] = dot_tn(left, mine)
    gram[HALF:, :] = dot_tn(right, mine)


def applied(pos, own, other, inv):
    left, right = halves(pos, own, other)
    new_left = dot_nt(left, inv[0:HALF, 0:HALF])
    new_right = dot_nt(left, inv[HALF:, 0:HALF]) + dot_nt(right, inv[HALF:, HALF:])
    return new_left, new_right


def apply_gram_kernel(pos, own, other, inv, out, out_other, gram):
    new_left, new_right = applied(pos, own, other, inv)
    first = pos[3] == 0
    mine = jnp.where(first, new_left, new_right)
    out[...] = mine
    out_other[...] = jnp.where(first, new_right, new_left)
    gram[0:HALF, :] = dot_tn(new_left, mine)
    gram[HALF:, :] = dot_tn(new_right, mine)


def make_apply_scaled(scale):
    def apply_scaled_kernel(pos, own, other, inv, out):
        new_left, new_right = applied(pos, own, other, inv)
        out[...] = jnp.where(pos[3] == 0, new_left, new_right) * F32(scale)

    return apply_scaled_kernel


AHEAD = 4


def inverse_factor(matrix):
    size = matrix.shape[0]
    blocks_n = size // 8
    lane = lax.broadcasted_iota(jnp.int32, (8, size), 1)
    sub = lax.broadcasted_iota(jnp.int32, (8, size), 0)

    def spread(column):
        return jnp.broadcast_to(column, (8, size))

    def body(step, array):
        blocks = [array[8 * b : 8 * b + 8, :] for b in range(blocks_n)]
        rest = size - 8 * step
        for start in range(0, 8, AHEAD):
            cols = [
                [spread(block[:, start + t : start + t + 1]) for block in blocks]
                for t in range(AHEAD)
            ]
            for t in range(AHEAD):
                j = start + t
                pivot = spread(cols[t][0][j : j + 1, :])
                root = lax.rsqrt(pivot)
                root = root * (1.5 - (0.5 * pivot * root) * root)
                line = jnp.where(lane == j, root, spread(blocks[0][j : j + 1, :]) * root)
                factors = [col * root for col in cols[t]]
                factors[0] = jnp.where(sub > j, factors[0], 0.0)
                for later in range(t + 1, AHEAD):
                    entry = spread(cols[later][0][j : j + 1, :]) * root
                    cols[later] = [c - f * entry for c, f in zip(cols[later], factors)]
                blocks = [jnp.where(lane == j, 0.0, b) - f * line for b, f in zip(blocks, factors)]
                done = jnp.where((lane > j) & (lane < rest), 0.0, line)
                blocks[0] = jnp.where(sub == j, done, blocks[0])
        turned = jnp.concatenate(blocks[1:] + blocks[:1], axis=0)
        return pltpu.roll(turned, size - 8, 1)

    return lax.fori_loop(0, blocks_n, body, matrix)


def factor_kernel(pos, own, other, inv):
    first = pos[3] == 0
    a, b = own[...], other[...]
    left = jnp.where(first, a, b)
    corner = jnp.where(first, b, a)[HALF:, :]
    inv_first = inverse_factor(left[0:HALF, :])
    below = left[HALF:, :]
    low = dot_nt(below, inv_first)
    inv_last = inverse_factor(corner - dot_nt(low, low))
    inv[0:HALF, 0:HALF] = inv_first
    inv[0:HALF, HALF:] = jnp.zeros((HALF, HALF), F32)
    inv[HALF:, 0:HALF] = -dot_nn(inv_last, dot_nn(low, inv_first))
    inv[HALF:, HALF:] = inv_last


def call(kernel, shapes, scalars, arrays, scratch=(), micros=2):
    smem = pl.BlockSpec(memory_space=pltpu.SMEM)
    vmem = pl.BlockSpec(memory_space=pltpu.VMEM)
    outs = [jax.ShapeDtypeStruct(shape, F32) for shape in shapes]
    result = pl.pallas_call(
        kernel,
        out_shape=outs,
        in_specs=[smem] * len(scalars) + [vmem] * len(arrays),
        out_specs=[vmem] * len(outs),
        scratch_shapes=[pltpu.VMEM(shape, F32) for shape in scratch],
        compiler_params=pltpu.CompilerParams(vmem_limit_bytes=VMEM_LIMIT),
        cost_estimate=pl.CostEstimate(
            flops=int(micros * 1e9), bytes_accessed=int(micros * 1e6), transcendentals=0
        ),
    )(*scalars, *arrays)
    return result


def ring(size, shift):
    return [(i, (i + shift) % size) for i in range(size)]


def send(value, axis, shift):
    size = {"y": NY, "z": NZ, "col": NX, "rep": 2}[axis]
    return lax.ppermute(value, axis, ring(size, shift))


def shards(tiles, block_row, block_col, live_rows, omega):
    local_tiles = tiles[0, 0]
    rows, cols, live = block_row[0, 0], block_col[0, 0], live_rows[0, 0]
    pos = jnp.stack([lax.axis_index(a) for a in ("y", "z", "col", "rep")]).astype(jnp.int32)
    big = CB_DEV // NY * BS

    def gather_panel(own):
        line = jnp.concatenate([own] + [send(own, "z", k) for k in range(1, NZ)], axis=0)
        return [line] + [send(line, "y", k) for k in range(1, NY)]

    def gather_rows(own):
        return [own] + [send(own, "col", k) for k in range(1, NX)]

    def forward(pieces):
        out = call(
            forward_kernel,
            [(ROWS_OWN, HALF)] * NX,
            [pos, rows, cols, live],
            [local_tiles, *pieces],
            [(CB_DEV * BS, HALF), (RB_DEV * BS, HALF)],
            5,
        )
        got = [out[0]] + [send(out[k], "col", k) for k in range(1, NX)]
        return call(sum_kernel, [(ROWS_OWN, HALF)], [], got, (), 1)[0]

    def backward(pieces):
        out = call(
            backward_kernel,
            [(big, HALF)] * NY,
            [pos, rows, cols, live],
            [local_tiles, *pieces],
            [(RB_DEV * BS, HALF), (CB_DEV * BS, HALF)],
            5,
        )
        got = [out[0]] + [send(out[k], "y", k) for k in range(1, NY)]
        parts = call(sum_split_kernel, [(COLS_OWN, HALF)] * NZ, [pos], got, (), 1)
        got = [parts[0]] + [send(parts[k], "z", k) for k in range(1, NZ)]
        return call(sum_kernel, [(COLS_OWN, HALF)], [], got, (), 1)[0]

    def sum_gram(gram):
        chunk = 2 * HALF // (NY * NX)
        parts = lax.all_to_all(gram.reshape(NY * NX, chunk, HALF), ("y", "col"), 0, 0)
        part = jnp.sum(parts, axis=0)
        parts = lax.all_to_all(jnp.broadcast_to(part[None], (NZ, chunk, HALF)), "z", 0, 0)
        part = jnp.sum(parts, axis=0)
        whole = lax.all_to_all(
            jnp.broadcast_to(part[None], (NY * NX, chunk, HALF)), ("y", "col"), 0, 0
        )
        return whole.reshape(2 * HALF, HALF)

    def factor(gram):
        mine = sum_gram(gram)
        other = send(mine, "rep", 1)
        return call(factor_kernel, [(2 * HALF, 2 * HALF)], [pos], [mine, other], (), 25)[0]

    def normalised(value, inv):
        other = send(value, "rep", 1)
        shape = value.shape
        return call(
            apply_gram_kernel, [shape, shape, (2 * HALF, HALF)], [pos], [value, other, inv]
        )

    def finished(value, other, inv, scale):
        return call(make_apply_scaled(scale), [value.shape], [pos], [value, other, inv])[0]

    own = forward(gather_panel(omega[0]))
    gram = call(gram_kernel, [(2 * HALF, HALF)], [pos], [own, send(own, "rep", 1)])[0]
    total_rows = ROWS_OWN * NX * NY * NZ
    total_cols = COLS_OWN * NX * NY * NZ
    for step in range(ITERS):
        pieces = gather_rows(own)
        inv = factor(gram)
        panel, panel_other, gram = normalised(backward(pieces), inv)
        pieces = gather_panel(panel)
        inv = factor(gram)
        if step == ITERS - 1:
            panel_basis = finished(panel, panel_other, inv, math.sqrt(total_cols))
        own, other, gram = normalised(forward(pieces), inv)
    basis = finished(own, other, factor(gram), math.sqrt(total_rows))
    return basis[None], panel_basis[None]


def solution(mesh):
    fine = Mesh(mesh.devices.reshape(NY, NZ, NX, 2), ("y", "z", "col", "rep"))
    row = ("y", "z")
    placed = (
        P(row, "col", None, None, None),
        P(row, "col", None),
        P(row, "col", None),
        P(row, "col", None),
        P("col", row, "rep"),
    )
    return jax.shard_map(
        shards,
        mesh=fine,
        in_specs=placed,
        out_specs=(P(row, "col", "rep"), P("col", row, "rep")),
        check_vma=False,
    )
```

```python
import math

import jax
import jax.numpy as jnp
from jax import lax
from jax.experimental import pallas as pl
from jax.experimental.pallas import tpu as pltpu
from jax.sharding import Mesh
from jax.sharding import PartitionSpec as P

ITERS = 2
RB_DEV = 24
CB_DEV = 40
BS = 128
HALF = 128
NY = 4
NZ = 8
NX = 4
ROWS_OWN = 768
COLS_OWN = 160
UNROLL = 4
F32 = jnp.float32
BF16 = jnp.bfloat16
VMEM_LIMIT = 40 * 1024 * 1024


def dot_nn(a, b):
    return lax.dot_general(
        a, b, (((1,), (0,)), ((), ())), precision=lax.Precision.HIGHEST, preferred_element_type=F32
    )


def dot_nt(a, b):
    return lax.dot_general(
        a, b, (((1,), (1,)), ((), ())), precision=lax.Precision.HIGHEST, preferred_element_type=F32
    )


def dot_tn(a, b):
    return lax.dot_general(
        a, b, (((0,), (0,)), ((), ())), precision=lax.Precision.HIGHEST, preferred_element_type=F32
    )


def split(x):
    high = x.astype(BF16)
    return high, (x - high.astype(F32)).astype(BF16)


def product_of(tile, block, dims):
    tile_high, tile_low = split(tile)
    high, low = split(block)

    def mul(a, b):
        return lax.dot_general(a, b, (dims, ((), ())), preferred_element_type=F32)

    return mul(tile_high, high) + (mul(tile_high, low) + mul(tile_low, high))


def masked_tile(tiles, slots, slot):
    iota = lax.broadcasted_iota(jnp.int32, (BS, BS), 0)
    return jnp.where(iota < slots[2, slot], tiles[slot], F32(0.0))


def block_at(index):
    return pl.ds(pl.multiple_of(index * BS, BS), BS)


def accumulate(slots, held, total, source, target, shift, count, tiles, dims):
    def body(step, carry):
        base = step * UNROLL
        products = []
        for offset in range(UNROLL):
            slot = base + offset
            tile = masked_tile(tiles, slots, slot)
            products.append(product_of(tile, held[block_at(slots[source, slot]), :], dims))
        for offset in range(UNROLL):
            place = lax.rem(slots[target, base + offset] + (count - shift), count)
            total[block_at(place), :] += products[offset]
        return carry

    total[...] = jnp.zeros_like(total)
    lax.fori_loop(0, tiles.shape[0] // UNROLL, body, 0)


def forward_kernel(
    pos, slots, tiles, line, before, after, far_a, far_b, carried, o0, o1, o2, o3, passed, held, total
):
    y, z, x = pos[0], pos[1], pos[2]
    passed[...] = carried[...]
    half = NZ // 2
    parts = [(0, line, 0), (NY - 1, before, 0), (1, after, 0), (2, far_a, 0), (2, far_b, half)]
    for shift, ref, first in parts:
        from_y = lax.rem(y + shift, NY)
        for k in range(ref.shape[0] // COLS_OWN):
            from_z = lax.rem(z + (half + first + k), NZ)
            place = pl.multiple_of((from_y * NZ + from_z) * COLS_OWN, 32)
            held[pl.ds(place, COLS_OWN), :] = ref[k * COLS_OWN : (k + 1) * COLS_OWN, :]
    accumulate(slots, held, total, 1, 0, x * (RB_DEV // NX), RB_DEV, tiles, ((1,), (0,)))
    for k, out in enumerate((o0, o1, o2, o3)):
        out[...] = total[k * ROWS_OWN : (k + 1) * ROWS_OWN, :]


def backward_kernel(
    pos, slots, tiles, p0, p1, p2, p3, carried, o0, o1, far_a, far_b, o3, passed, held, total
):
    y, x = pos[0], pos[2]
    passed[...] = carried[...]
    for j, piece in enumerate((p0, p1, p2, p3)):
        from_x = lax.rem(x + (NX - j), NX)
        held[pl.ds(pl.multiple_of(from_x * ROWS_OWN, 256), ROWS_OWN), :] = piece[...]
    accumulate(slots, held, total, 0, 1, y * (CB_DEV // NY), CB_DEV, tiles, ((0,), (0,)))
    start = 0
    for out in (o0, o1, far_a, far_b, o3):
        out[...] = total[start : start + out.shape[0], :]
        start += out.shape[0]


def join_kernel(*refs):
    *pieces, carried, line, passed = refs
    passed[...] = carried[...]
    start = 0
    for piece in pieces:
        line[start : start + piece.shape[0], :] = piece[...]
        start += piece.shape[0]


def cut_kernel(before, after, carried, first, last, passed):
    passed[...] = carried[...]
    size = first.shape[0]
    first[...] = before[0:size, :]
    last[...] = after[size:, :]


def relay_y_kernel(near, far_a, back, far_b, carried, to_near, to_back, passed):
    passed[...] = carried[...]
    size = far_a.shape[0]
    to_near[0:size, :] = near[0:size, :] + far_a[...]
    to_near[size:, :] = near[size:, :]
    to_back[0:size, :] = back[0:size, :]
    to_back[size:, :] = back[size:, :] + far_b[...]


def split_z_kernel(pos, own, before, after, carried, up, down, mine, near, back, passed):
    passed[...] = carried[...]
    z = pos[1]

    def piece(shift):
        place = pl.ds(pl.multiple_of(lax.rem(z + shift, NZ) * COLS_OWN, 32), COLS_OWN)
        return own[place, :] + (before[place, :] + after[place, :])

    for k, shift in enumerate((2, 3, 4)):
        up[k * COLS_OWN : (k + 1) * COLS_OWN, :] = piece(shift)
    for k, shift in enumerate((5, 6)):
        down[k * COLS_OWN : (k + 1) * COLS_OWN, :] = piece(shift)
    mine[...] = piece(0)
    near[...] = piece(1)
    back[...] = piece(NZ - 1)


def relay_z_kernel(mine, near, back, up, down, before, to_mine, to_near, to_back):
    to_back[...] = back[...] + up[0:COLS_OWN, :]
    to_mine[...] = mine[...] + (up[COLS_OWN : 2 * COLS_OWN, :] + down[0:COLS_OWN, :])
    to_near[...] = near[...] + (up[2 * COLS_OWN :, :] + down[COLS_OWN:, :])


def sum_kernel(a, b, c, d, before, out):
    out[...] = (a[...] + c[...]) + (b[...] + d[...])


def sum_three_kernel(a, b, c, out):
    out[...] = a[...] + (b[...] + c[...])


def halves(pos, own, other):
    first = pos[3] == 0
    a, b = own[...], other[...]
    return jnp.where(first, a, b), jnp.where(first, b, a)


def gram_kernel(pos, own, other, gram):
    left, right = halves(pos, own, other)
    mine = own[...]
    gram[0:HALF, :] = dot_tn(left, mine)
    gram[HALF:, :] = dot_tn(right, mine)


def applied(pos, own, other, inv):
    left, right = halves(pos, own, other)
    new_left = dot_nt(left, inv[0:HALF, 0:HALF])
    new_right = dot_nt(left, inv[HALF:, 0:HALF]) + dot_nt(right, inv[HALF:, HALF:])
    return new_left, new_right


def apply_gram_kernel(pos, own, other, inv, out, out_other, gram):
    new_left, new_right = applied(pos, own, other, inv)
    first = pos[3] == 0
    mine = jnp.where(first, new_left, new_right)
    out[...] = mine
    out_other[...] = jnp.where(first, new_right, new_left)
    gram[0:HALF, :] = dot_tn(new_left, mine)
    gram[HALF:, :] = dot_tn(new_right, mine)


def make_apply_scaled(scale):
    def apply_scaled_kernel(pos, own, other, inv, out):
        new_left, new_right = applied(pos, own, other, inv)
        out[...] = jnp.where(pos[3] == 0, new_left, new_right) * F32(scale)

    return apply_scaled_kernel


AHEAD = 4


def inverse_factor(matrix):
    size = matrix.shape[0]
    blocks_n = size // 8
    lane = lax.broadcasted_iota(jnp.int32, (8, size), 1)
    sub = lax.broadcasted_iota(jnp.int32, (8, size), 0)

    def spread(column):
        return jnp.broadcast_to(column, (8, size))

    def body(step, array):
        blocks = [array[8 * b : 8 * b + 8, :] for b in range(blocks_n)]
        rest = size - 8 * step
        for start in range(0, 8, AHEAD):
            cols = [
                [spread(block[:, start + t : start + t + 1]) for block in blocks]
                for t in range(AHEAD)
            ]
            for t in range(AHEAD):
                j = start + t
                pivot = spread(cols[t][0][j : j + 1, :])
                root = lax.rsqrt(pivot)
                root = root * (1.5 - (0.5 * pivot * root) * root)
                line = jnp.where(lane == j, root, spread(blocks[0][j : j + 1, :]) * root)
                factors = [col * root for col in cols[t]]
                factors[0] = jnp.where(sub > j, factors[0], 0.0)
                for later in range(t + 1, AHEAD):
                    entry = spread(cols[later][0][j : j + 1, :]) * root
                    cols[later] = [c - f * entry for c, f in zip(cols[later], factors)]
                blocks = [jnp.where(lane == j, 0.0, b) - f * line for b, f in zip(blocks, factors)]
                done = jnp.where((lane > j) & (lane < rest), 0.0, line)
                blocks[0] = jnp.where(sub == j, done, blocks[0])
        turned = jnp.concatenate(blocks[1:] + blocks[:1], axis=0)
        return pltpu.roll(turned, size - 8, 1)

    return lax.fori_loop(0, blocks_n, body, matrix)


def factor_kernel(pos, own, other, inv):
    first = pos[3] == 0
    a, b = own[...], other[...]
    left = jnp.where(first, a, b)
    corner = jnp.where(first, b, a)[HALF:, :]
    inv_first = inverse_factor(left[0:HALF, :])
    below = left[HALF:, :]
    low = dot_nt(below, inv_first)
    inv_last = inverse_factor(corner - dot_nt(low, low))
    inv[0:HALF, 0:HALF] = inv_first
    inv[0:HALF, HALF:] = jnp.zeros((HALF, HALF), F32)
    inv[HALF:, 0:HALF] = -dot_nn(inv_last, dot_nn(low, inv_first))
    inv[HALF:, HALF:] = inv_last


def call(kernel, shapes, scalars, arrays, scratch=(), before=()):
    smem = pl.BlockSpec(memory_space=pltpu.SMEM)
    vmem = pl.BlockSpec(memory_space=pltpu.VMEM)
    anywhere = pl.BlockSpec(memory_space=pl.ANY)
    return pl.pallas_call(
        kernel,
        out_shape=[jax.ShapeDtypeStruct(shape, F32) for shape in shapes],
        in_specs=[smem] * len(scalars) + [vmem] * len(arrays) + [anywhere] * len(before),
        out_specs=[vmem] * len(shapes),
        scratch_shapes=[pltpu.VMEM(shape, F32) for shape in scratch],
        compiler_params=pltpu.CompilerParams(vmem_limit_bytes=VMEM_LIMIT),
        cost_estimate=pl.CostEstimate(flops=1000000, bytes_accessed=100000, transcendentals=0),
    )(*scalars, *arrays, *before)


def ring(size, shift):
    return [(i, (i + shift) % size) for i in range(size)]


def send(value, axis, shift):
    size = {"y": NY, "z": NZ, "col": NX, "rep": 2}[axis]
    return lax.ppermute(value, axis, ring(size, shift))


def shards(tiles, block_row, block_col, live_rows, omega):
    local_tiles = tiles[0, 0]
    slots = jnp.concatenate([block_row[0], block_col[0], live_rows[0]], axis=0)
    pos = jnp.stack([lax.axis_index(a) for a in ("y", "z", "col", "rep")]).astype(jnp.int32)
    big = CB_DEV // NY * BS
    grams = (2 * HALF, HALF)

    def sum_ring(value, axis, before=pos):
        got = [value] + [send(value, axis, k) for k in range(1, 4)]
        return call(sum_kernel, [value.shape], [], got, (), [before])[0]

    def scatter_z(gram):
        parts = lax.all_to_all(gram.reshape(NZ, 2 * HALF // NZ, HALF), "z", 0, 0)
        return jnp.sum(parts, axis=0)

    def spread_z(part):
        whole = lax.all_to_all(jnp.broadcast_to(part[None], (NZ, *part.shape)), "z", 0, 0)
        return whole.reshape(grams)

    def gather_panel(own, gram=None):
        carried = own[0:8] if gram is None else sum_ring(sum_ring(gram, "y"), "col")
        up, down = send(own, "z", 1), send(own, "z", NZ - 1)
        three = jnp.concatenate([up, own, down], axis=0)
        far_up, far_down = send(three, "z", 3), send(three[: 2 * COLS_OWN], "z", NZ - 3)
        line, carried = call(
            join_kernel, [(big, HALF), carried.shape], [], [far_up, up, own, down, far_down, carried]
        )
        before, after = send(line, "y", 1), send(line, "y", NY - 1)
        if gram is not None:
            carried = scatter_z(carried)
        first, last, carried = call(
            cut_kernel, [(big // 2, HALF)] * 2 + [carried.shape], [], [before, after, carried]
        )
        far_a, far_b = send(first, "y", 1), send(last, "y", NY - 1)
        if gram is not None:
            carried = spread_z(carried)
        return [line, before, after, far_a, far_b], carried

    def gather_rows(own):
        return [own] + [send(own, "col", k) for k in range(1, NX)]

    def forward(pieces, carried):
        *out, passed = call(
            forward_kernel,
            [(ROWS_OWN, HALF)] * NX + [carried.shape],
            [pos, slots],
            [local_tiles, *pieces, carried],
            [(CB_DEV * BS, HALF), (RB_DEV * BS, HALF)],
        )
        return [out[0]] + [send(out[k], "col", k) for k in range(1, NX)], passed

    def forward_sum(got, before):
        return call(sum_kernel, [(ROWS_OWN, HALF)], [], got, (), [before])[0]

    def backward(pieces, gram):
        part = scatter_z(sum_ring(gram, "y"))
        own, near, far_a, far_b, back, part = call(
            backward_kernel,
            [(big, HALF)] * 2 + [(big // 2, HALF)] * 2 + [(big, HALF), part.shape],
            [pos, slots],
            [local_tiles, *pieces, part],
            [(RB_DEV * BS, HALF), (CB_DEV * BS, HALF)],
        )
        far_a, far_b = send(far_a, "y", 1), send(far_b, "y", NY - 1)
        part = sum_ring(part, "col")
        near, back, part = call(
            relay_y_kernel, [(big, HALF)] * 2 + [part.shape], [], [near, far_a, back, far_b, part]
        )
        before, after = send(near, "y", 1), send(back, "y", NY - 1)
        mine = spread_z(part)
        other = send(mine, "rep", 1)
        piece = (COLS_OWN, HALF)
        up, down, own, near, back, other = call(
            split_z_kernel,
            [(3 * COLS_OWN, HALF), (2 * COLS_OWN, HALF), piece, piece, piece, grams],
            [pos],
            [own, before, after, other],
        )
        up, down = send(up, "z", 3), send(down, "z", NZ - 3)
        inv = factor(mine, other)
        own, near, back = call(
            relay_z_kernel, [piece] * 3, [], [own, near, back, up, down], (), [inv]
        )
        got = [own, send(near, "z", 1), send(back, "z", NZ - 1)]
        return call(sum_three_kernel, [piece], [], got)[0], inv

    def sum_gram(gram):
        count, chunk = NY * NX, 2 * HALF // (NY * NX)
        parts = lax.all_to_all(gram.reshape(count, chunk, HALF), ("y", "col"), 0, 0)
        part = jnp.sum(parts, axis=0)
        parts = lax.all_to_all(jnp.broadcast_to(part[None], (NZ, chunk, HALF)), "z", 0, 0)
        part = jnp.sum(parts, axis=0)
        whole = lax.all_to_all(
            jnp.broadcast_to(part[None], (count, chunk, HALF)), ("y", "col"), 0, 0
        )
        return whole.reshape(grams)

    def factor(mine, other):
        return call(factor_kernel, [(2 * HALF, 2 * HALF)], [pos], [mine, other])[0]

    def normalised(value, inv):
        other = send(value, "rep", 1)
        shape = value.shape
        return call(apply_gram_kernel, [shape, shape, grams], [pos], [value, other, inv])

    def finished(value, other, inv, scale):
        return call(make_apply_scaled(scale), [value.shape], [pos], [value, other, inv])[0]

    got, _ = forward(*gather_panel(omega[0]))
    own = forward_sum(got, pos)
    gram = call(gram_kernel, [grams], [pos], [own, send(own, "rep", 1)])[0]
    total_rows = ROWS_OWN * NX * NY * NZ
    total_cols = COLS_OWN * NX * NY * NZ
    for step in range(ITERS):
        value, inv = backward(gather_rows(own), gram)
        panel, panel_other, gram = normalised(value, inv)
        pieces, mine = gather_panel(panel, gram)
        got, other = forward(pieces, send(mine, "rep", 1))
        inv = factor(mine, other)
        if step == ITERS - 1:
            panel_basis = finished(panel, panel_other, inv, math.sqrt(total_cols))
        own, other, gram = normalised(forward_sum(got, inv), inv)
    mine = sum_gram(gram)
    inv = factor(mine, send(mine, "rep", 1))
    basis = finished(own, other, inv, math.sqrt(total_rows))
    return basis[None], panel_basis[None]


def solution(mesh):
    fine = Mesh(mesh.devices.reshape(NY, NZ, NX, 2), ("y", "z", "col", "rep"))
    row = ("y", "z")
    placed = (
        P(row, "col", None, None, None),
        P(row, "col", None),
        P(row, "col", None),
        P(row, "col", None),
        P("col", row, "rep"),
    )
    return jax.shard_map(
        shards,
        mesh=fine,
        in_specs=placed,
        out_specs=(P(row, "col", "rep"), P("col", row, "rep")),
        check_vma=False,
    )
```

```python
import math

import jax
import jax.numpy as jnp
from jax import lax
from jax.experimental import pallas as pl
from jax.experimental.pallas import tpu as pltpu
from jax.sharding import Mesh
from jax.sharding import PartitionSpec as P

ITERS = 2
RB_DEV = 24
CB_DEV = 40
BS = 128
HALF = 128
NY = 4
NZ = 8
NX = 4
ROWS_OWN = 768
COLS_OWN = 160
UNROLL = 4
F32 = jnp.float32
BF16 = jnp.bfloat16
VMEM_LIMIT = 16 * 1024 * 1024


def dot_nn(a, b):
    return lax.dot_general(
        a, b, (((1,), (0,)), ((), ())), precision=lax.Precision.HIGHEST, preferred_element_type=F32
    )


def dot_nt(a, b):
    return lax.dot_general(
        a, b, (((1,), (1,)), ((), ())), precision=lax.Precision.HIGHEST, preferred_element_type=F32
    )


def dot_tn(a, b):
    return lax.dot_general(
        a, b, (((0,), (0,)), ((), ())), precision=lax.Precision.HIGHEST, preferred_element_type=F32
    )


def split(x):
    high = x.astype(BF16)
    return high, (x - high.astype(F32)).astype(BF16)


def product_of(tile, block, dims):
    tile_high, tile_low = split(tile)
    high, low = split(block)

    def mul(a, b):
        return lax.dot_general(a, b, (dims, ((), ())), preferred_element_type=F32)

    return mul(tile_high, high) + (mul(tile_high, low) + mul(tile_low, high))


def masked_tile(tiles, slots, slot):
    iota = lax.broadcasted_iota(jnp.int32, (BS, BS), 0)
    return jnp.where(iota < slots[2, slot], tiles[slot], F32(0.0))


def block_at(index):
    return pl.ds(pl.multiple_of(index * BS, BS), BS)


def accumulate(slots, held, total, source, target, shift, count, tiles, dims):
    def body(step, carry):
        base = step * UNROLL
        products = []
        for offset in range(UNROLL):
            slot = base + offset
            tile = masked_tile(tiles, slots, slot)
            products.append(product_of(tile, held[block_at(slots[source, slot]), :], dims))
        for offset in range(UNROLL):
            place = lax.rem(slots[target, base + offset] + (count - shift), count)
            total[block_at(place), :] += products[offset]
        return carry

    total[...] = jnp.zeros_like(total)
    lax.fori_loop(0, tiles.shape[0] // UNROLL, body, 0)


def forward_kernel(
    pos, slots, tiles, line, before, after, far_a, far_b, carried, o0, o1, o2, o3, passed, held, total
):
    y, z, x = pos[0], pos[1], pos[2]
    passed[...] = carried[...]
    half = NZ // 2
    parts = [(0, line, 0), (NY - 1, before, 0), (1, after, 0), (2, far_a, 0), (2, far_b, half)]
    for shift, ref, first in parts:
        from_y = lax.rem(y + shift, NY)
        for k in range(ref.shape[0] // COLS_OWN):
            from_z = lax.rem(z + (half + first + k), NZ)
            place = pl.multiple_of((from_y * NZ + from_z) * COLS_OWN, 32)
            held[pl.ds(place, COLS_OWN), :] = ref[k * COLS_OWN : (k + 1) * COLS_OWN, :]
    accumulate(slots, held, total, 1, 0, x * (RB_DEV // NX), RB_DEV, tiles, ((1,), (0,)))
    for k, out in enumerate((o0, o1, o2, o3)):
        out[...] = total[k * ROWS_OWN : (k + 1) * ROWS_OWN, :]


def backward_kernel(
    pos, slots, tiles, p0, p1, p2, p3, carried, o0, o1, far_a, far_b, o3, passed, held, total
):
    y, x = pos[0], pos[2]
    passed[...] = carried[...]
    for j, piece in enumerate((p0, p1, p2, p3)):
        from_x = lax.rem(x + (NX - j), NX)
        held[pl.ds(pl.multiple_of(from_x * ROWS_OWN, 256), ROWS_OWN), :] = piece[...]
    accumulate(slots, held, total, 0, 1, y * (CB_DEV // NY), CB_DEV, tiles, ((0,), (0,)))
    start = 0
    for out in (o0, o1, far_a, far_b, o3):
        out[...] = total[start : start + out.shape[0], :]
        start += out.shape[0]


def join_kernel(*refs):
    *pieces, carried, line, passed = refs
    passed[...] = carried[...]
    start = 0
    for piece in pieces:
        line[start : start + piece.shape[0], :] = piece[...]
        start += piece.shape[0]


def fan_kernel(up, own, down, three, two):
    three[0:COLS_OWN, :] = up[...]
    three[COLS_OWN : 2 * COLS_OWN, :] = own[...]
    three[2 * COLS_OWN :, :] = down[...]
    two[0:COLS_OWN, :] = up[...]
    two[COLS_OWN:, :] = own[...]


def cut_kernel(before, after, parts, first, last, copies):
    size = first.shape[0]
    first[...] = before[0:size, :]
    last[...] = after[size:, :]
    total = parts[0]
    for k in range(1, parts.shape[0]):
        total = total + parts[k]
    for k in range(copies.shape[0]):
        copies[k] = total


def relay_y_kernel(near, far_a, back, far_b, a, b, c, d, to_near, to_back, copies):
    total = (a[...] + c[...]) + (b[...] + d[...])
    for k in range(copies.shape[0]):
        copies[k] = total
    size = far_a.shape[0]
    to_near[0:size, :] = near[0:size, :] + far_a[...]
    to_near[size:, :] = near[size:, :]
    to_back[0:size, :] = back[0:size, :]
    to_back[size:, :] = back[size:, :] + far_b[...]


def split_z_kernel(pos, own, before, after, carried, up, down, mine, near, back, passed):
    passed[...] = carried[...]
    z = pos[1]

    def piece(shift):
        place = pl.ds(pl.multiple_of(lax.rem(z + shift, NZ) * COLS_OWN, 32), COLS_OWN)
        return own[place, :] + (before[place, :] + after[place, :])

    for k, shift in enumerate((2, 3, 4)):
        up[k * COLS_OWN : (k + 1) * COLS_OWN, :] = piece(shift)
    for k, shift in enumerate((5, 6)):
        down[k * COLS_OWN : (k + 1) * COLS_OWN, :] = piece(shift)
    mine[...] = piece(0)
    near[...] = piece(1)
    back[...] = piece(NZ - 1)


def relay_z_kernel(mine, near, back, up, down, before, to_mine, to_near, to_back):
    to_back[...] = back[...] + up[0:COLS_OWN, :]
    to_mine[...] = mine[...] + (up[COLS_OWN : 2 * COLS_OWN, :] + down[0:COLS_OWN, :])
    to_near[...] = near[...] + (up[2 * COLS_OWN :, :] + down[COLS_OWN:, :])


def sum_kernel(a, b, c, d, before, out):
    out[...] = (a[...] + c[...]) + (b[...] + d[...])


def sum_three_kernel(a, b, c, out):
    out[...] = a[...] + (b[...] + c[...])


def halves(pos, own, other):
    first = pos[3] == 0
    a, b = own[...], other[...]
    return jnp.where(first, a, b), jnp.where(first, b, a)


def gram_kernel(pos, own, other, gram):
    left, right = halves(pos, own, other)
    mine = own[...]
    gram[0:HALF, :] = dot_tn(left, mine)
    gram[HALF:, :] = dot_tn(right, mine)


def applied(pos, own, other, inv):
    left, right = halves(pos, own, other)
    new_left = dot_nt(left, inv[0:HALF, 0:HALF])
    new_right = dot_nt(left, inv[HALF:, 0:HALF]) + dot_nt(right, inv[HALF:, HALF:])
    return new_left, new_right


def apply_gram_kernel(pos, own, other, inv, out, out_other, gram):
    new_left, new_right = applied(pos, own, other, inv)
    first = pos[3] == 0
    mine = jnp.where(first, new_left, new_right)
    out[...] = mine
    out_other[...] = jnp.where(first, new_right, new_left)
    gram[0:HALF, :] = dot_tn(new_left, mine)
    gram[HALF:, :] = dot_tn(new_right, mine)


def make_apply_scaled(scale):
    def apply_scaled_kernel(pos, own, other, inv, out):
        new_left, new_right = applied(pos, own, other, inv)
        out[...] = jnp.where(pos[3] == 0, new_left, new_right) * F32(scale)

    return apply_scaled_kernel


WIDE = 16


def thirds(x):
    high = x.astype(BF16).astype(F32)
    rest = x - high
    middle = rest.astype(BF16).astype(F32)
    return high, middle, rest - middle


def inverse_factor(matrix):
    size = matrix.shape[0]
    lane = lax.broadcasted_iota(jnp.int32, (WIDE, size), 1)
    sub = lax.broadcasted_iota(jnp.int32, (WIDE, size), 0)
    all_lanes = lax.broadcasted_iota(jnp.int32, (size, size), 1)

    def spread(column):
        return jnp.broadcast_to(column, (WIDE, size))

    def body(step, array):
        rest = size - WIDE * step
        top = array[0:WIDE, :]
        cols = [spread(top[:, j : j + 1]) for j in range(WIDE)]
        upper = jnp.zeros((WIDE, size), F32)
        for j in range(WIDE):
            root = lax.rsqrt(spread(cols[j][j : j + 1, :]))
            line = jnp.where(lane == j, root, spread(top[j : j + 1, :]) * root)
            factor = jnp.where(sub > j, cols[j] * root, 0.0)
            for later in range(j + 1, WIDE):
                entry = spread(cols[later][j : j + 1, :]) * root
                cols[later] = cols[later] - factor * entry
            top = jnp.where((lane == j) & (sub > j), 0.0, top) - factor * line
            upper = jnp.where(sub == j, line, upper)
        done = jnp.where((lane > sub) & (lane < rest), 0.0, upper)
        a, b, c = thirds(jnp.where((lane >= WIDE) & (lane < rest), upper, 0.0))
        p, q, r = thirds(jnp.where((lane < WIDE) & (lane > sub), 0.0, upper))
        left = jnp.concatenate([a, a, b, a, b, c], axis=0).astype(BF16)
        right = jnp.concatenate([p, q, p, r, q, p], axis=0).astype(BF16)
        change = lax.dot_general(
            left, right, (((0,), (0,)), ((), ())), preferred_element_type=F32
        )
        array = jnp.where(all_lanes < WIDE, 0.0, array) - change
        return pltpu.roll(jnp.concatenate([array[WIDE:], done], axis=0), size - WIDE, 1)

    return lax.fori_loop(0, size // WIDE, body, matrix)


def factor_kernel(pos, own, other, inv):
    first = pos[3] == 0
    a, b = own[...], other[...]
    left = jnp.where(first, a, b)
    corner = jnp.where(first, b, a)[HALF:, :]
    inv_first = inverse_factor(left[0:HALF, :])
    below = left[HALF:, :]
    low = dot_nt(below, inv_first)
    inv_last = inverse_factor(corner - dot_nt(low, low))
    inv[0:HALF, 0:HALF] = inv_first
    inv[0:HALF, HALF:] = jnp.zeros((HALF, HALF), F32)
    inv[HALF:, 0:HALF] = -dot_nn(inv_last, dot_nn(low, inv_first))
    inv[HALF:, HALF:] = inv_last


def call(kernel, shapes, scalars, arrays, scratch=(), before=()):
    smem = pl.BlockSpec(memory_space=pltpu.SMEM)
    vmem = pl.BlockSpec(memory_space=pltpu.VMEM)
    anywhere = pl.BlockSpec(memory_space=pl.ANY)
    return pl.pallas_call(
        kernel,
        out_shape=[jax.ShapeDtypeStruct(shape, F32) for shape in shapes],
        in_specs=[smem] * len(scalars) + [vmem] * len(arrays) + [anywhere] * len(before),
        out_specs=[vmem] * len(shapes),
        scratch_shapes=[pltpu.VMEM(shape, F32) for shape in scratch],
        compiler_params=pltpu.CompilerParams(vmem_limit_bytes=VMEM_LIMIT),
        cost_estimate=pl.CostEstimate(flops=1000000, bytes_accessed=100000, transcendentals=0),
    )(*scalars, *arrays, *before)


def ring(size, shift):
    return [(i, (i + shift) % size) for i in range(size)]


def send(value, axis, shift):
    size = {"y": NY, "z": NZ, "col": NX, "rep": 2}[axis]
    return lax.ppermute(value, axis, ring(size, shift))


def shards(tiles, block_row, block_col, live_rows, omega):
    local_tiles = tiles[0, 0]
    slots = jnp.concatenate([block_row[0], block_col[0], live_rows[0]], axis=0)
    pos = jnp.stack([lax.axis_index(a) for a in ("y", "z", "col", "rep")]).astype(jnp.int32)
    big = CB_DEV // NY * BS
    grams = (2 * HALF, HALF)
    chunks = (NZ, 2 * HALF // NZ, HALF)

    def sum_ring(value, axis, before=pos):
        got = [value] + [send(value, axis, k) for k in range(1, 4)]
        return call(sum_kernel, [value.shape], [], got, (), [before])[0]

    def exchange_z(parts):
        return lax.all_to_all(parts, "z", 0, 0)

    def gather_panel(own, gram=None):
        carried = own[0:8] if gram is None else sum_ring(sum_ring(gram, "y"), "col")
        up, down = send(own, "z", 1), send(own, "z", NZ - 1)
        three, two = call(
            fan_kernel, [(3 * COLS_OWN, HALF), (2 * COLS_OWN, HALF)], [], [up, own, down]
        )
        far_up, far_down = send(three, "z", 3), send(two, "z", NZ - 3)
        line, carried = call(
            join_kernel, [(big, HALF), carried.shape], [], [far_up, up, own, down, far_down, carried]
        )
        before, after = send(line, "y", 1), send(line, "y", NY - 1)
        if gram is None:
            parts = carried.reshape(1, *carried.shape)
        else:
            parts = exchange_z(carried.reshape(chunks))
        first, last, copies = call(
            cut_kernel, [(big // 2, HALF)] * 2 + [parts.shape], [], [before, after, parts]
        )
        far_a, far_b = send(first, "y", 1), send(last, "y", NY - 1)
        if gram is None:
            return [line, before, after, far_a, far_b], carried
        return [line, before, after, far_a, far_b], exchange_z(copies).reshape(grams)

    def gather_rows(own):
        return [own] + [send(own, "col", k) for k in range(1, NX)]

    def forward(pieces, carried):
        *out, passed = call(
            forward_kernel,
            [(ROWS_OWN, HALF)] * NX + [carried.shape],
            [pos, slots],
            [local_tiles, *pieces, carried],
            [(CB_DEV * BS, HALF), (RB_DEV * BS, HALF)],
        )
        return [out[0]] + [send(out[k], "col", k) for k in range(1, NX)], passed

    def forward_sum(got, before):
        return call(sum_kernel, [(ROWS_OWN, HALF)], [], got, (), [before])[0]

    def backward(pieces, gram):
        part = sum_ring(jnp.sum(exchange_z(gram.reshape(chunks)), axis=0), "y")
        own, near, far_a, far_b, back, part = call(
            backward_kernel,
            [(big, HALF)] * 2 + [(big // 2, HALF)] * 2 + [(big, HALF), part.shape],
            [pos, slots],
            [local_tiles, *pieces, part],
            [(RB_DEV * BS, HALF), (CB_DEV * BS, HALF)],
        )
        far_a, far_b = send(far_a, "y", 1), send(far_b, "y", NY - 1)
        parts = [part] + [send(part, "col", k) for k in range(1, NX)]
        near, back, copies = call(
            relay_y_kernel, [(big, HALF)] * 2 + [chunks], [], [near, far_a, back, far_b, *parts]
        )
        before, after = send(near, "y", 1), send(back, "y", NY - 1)
        mine = exchange_z(copies).reshape(grams)
        other = send(mine, "rep", 1)
        piece = (COLS_OWN, HALF)
        up, down, own, near, back, other = call(
            split_z_kernel,
            [(3 * COLS_OWN, HALF), (2 * COLS_OWN, HALF), piece, piece, piece, grams],
            [pos],
            [own, before, after, other],
        )
        up, down = send(up, "z", 3), send(down, "z", NZ - 3)
        inv = factor(mine, other)
        own, near, back = call(
            relay_z_kernel, [piece] * 3, [], [own, near, back, up, down], (), [inv]
        )
        got = [own, send(near, "z", 1), send(back, "z", NZ - 1)]
        return call(sum_three_kernel, [piece], [], got)[0], inv

    def sum_gram(gram):
        count, chunk = NY * NX, 2 * HALF // (NY * NX)
        parts = lax.all_to_all(gram.reshape(count, chunk, HALF), ("y", "col"), 0, 0)
        part = jnp.sum(parts, axis=0)
        parts = lax.all_to_all(jnp.broadcast_to(part[None], (NZ, chunk, HALF)), "z", 0, 0)
        part = jnp.sum(parts, axis=0)
        whole = lax.all_to_all(
            jnp.broadcast_to(part[None], (count, chunk, HALF)), ("y", "col"), 0, 0
        )
        return whole.reshape(grams)

    def factor(mine, other):
        return call(factor_kernel, [(2 * HALF, 2 * HALF)], [pos], [mine, other])[0]

    def normalised(value, inv):
        other = send(value, "rep", 1)
        shape = value.shape
        return call(apply_gram_kernel, [shape, shape, grams], [pos], [value, other, inv])

    def finished(value, other, inv, scale):
        return call(make_apply_scaled(scale), [value.shape], [pos], [value, other, inv])[0]

    got, _ = forward(*gather_panel(omega[0]))
    own = forward_sum(got, pos)
    gram = call(gram_kernel, [grams], [pos], [own, send(own, "rep", 1)])[0]
    total_rows = ROWS_OWN * NX * NY * NZ
    total_cols = COLS_OWN * NX * NY * NZ
    for step in range(ITERS):
        value, inv = backward(gather_rows(own), gram)
        panel, panel_other, gram = normalised(value, inv)
        pieces, mine = gather_panel(panel, gram)
        got, other = forward(pieces, send(mine, "rep", 1))
        inv = factor(mine, other)
        if step == ITERS - 1:
            panel_basis = finished(panel, panel_other, inv, math.sqrt(total_cols))
        own, other, gram = normalised(forward_sum(got, inv), inv)
    mine = sum_gram(gram)
    inv = factor(mine, send(mine, "rep", 1))
    basis = finished(own, other, inv, math.sqrt(total_rows))
    return basis[None], panel_basis[None]


def solution(mesh):
    fine = Mesh(mesh.devices.reshape(NY, NZ, NX, 2), ("y", "z", "col", "rep"))
    row = ("y", "z")
    placed = (
        P(row, "col", None, None, None),
        P(row, "col", None),
        P(row, "col", None),
        P(row, "col", None),
        P("col", row, "rep"),
    )
    return jax.shard_map(
        shards,
        mesh=fine,
        in_specs=placed,
        out_specs=(P(row, "col", "rep"), P("col", row, "rep")),
        check_vma=False,
    )
```

```python
import math

import jax
import jax.numpy as jnp
from jax import lax
from jax.experimental import pallas as pl
from jax.experimental.pallas import tpu as pltpu
from jax.sharding import Mesh
from jax.sharding import PartitionSpec as P

ITERS = 2
RB_DEV = 24
CB_DEV = 40
BS = 128
HALF = 128
NY = 4
NZ = 8
NX = 4
ROWS_OWN = 768
COLS_OWN = 160
UNROLL = 8
F32 = jnp.float32
BF16 = jnp.bfloat16
VMEM_LIMIT = 16 * 1024 * 1024


def dot_nn(a, b):
    return lax.dot_general(
        a, b, (((1,), (0,)), ((), ())), precision=lax.Precision.HIGHEST, preferred_element_type=F32
    )


def dot_nt(a, b):
    return lax.dot_general(
        a, b, (((1,), (1,)), ((), ())), precision=lax.Precision.HIGHEST, preferred_element_type=F32
    )


def dot_tn(a, b):
    return lax.dot_general(
        a, b, (((0,), (0,)), ((), ())), precision=lax.Precision.HIGHEST, preferred_element_type=F32
    )


def split(x):
    high = x.astype(BF16)
    return high, (x - high.astype(F32)).astype(BF16)


def product_of(a, b, dims):
    (axis_a,), (axis_b,) = dims
    pair = jnp.concatenate(split(b), axis=1 - axis_b)
    both = lax.dot_general(
        jnp.concatenate(split(a), axis=axis_a),
        jnp.concatenate([pair, pair], axis=axis_b),
        (dims, ((), ())),
        preferred_element_type=F32,
    )
    return both[:, :HALF] + both[:, HALF:]


def masked_tile(tiles, slots, slot):
    iota = lax.broadcasted_iota(jnp.int32, (BS, BS), 0)
    return jnp.where(iota < slots[2, slot], tiles[slot], F32(0.0))


def block_at(index):
    return pl.ds(pl.multiple_of(index * BS, BS), BS)


def accumulate(slots, held, total, source, target, shift, count, tiles, dims):
    def body(step, carry):
        base = step * UNROLL
        products = []
        for offset in range(UNROLL):
            slot = base + offset
            tile = masked_tile(tiles, slots, slot)
            products.append(product_of(tile, held[block_at(slots[source, slot]), :], dims))
        for offset in range(UNROLL):
            place = lax.rem(slots[target, base + offset] + (count - shift), count)
            total[block_at(place), :] += products[offset]
        return carry

    total[...] = jnp.zeros_like(total)
    lax.fori_loop(0, tiles.shape[0] // UNROLL, body, 0)


def forward_kernel(
    pos, slots, tiles, line, before, after, far_a, far_b, carried, o0, o1, o2, o3, passed, held, total
):
    y, z, x = pos[0], pos[1], pos[2]
    passed[...] = carried[...]
    half = NZ // 2
    parts = [(0, line, 0), (NY - 1, before, 0), (1, after, 0), (2, far_a, 0), (2, far_b, half)]
    for shift, ref, first in parts:
        from_y = lax.rem(y + shift, NY)
        for k in range(ref.shape[0] // COLS_OWN):
            from_z = lax.rem(z + (half + first + k), NZ)
            place = pl.multiple_of((from_y * NZ + from_z) * COLS_OWN, 32)
            held[pl.ds(place, COLS_OWN), :] = ref[k * COLS_OWN : (k + 1) * COLS_OWN, :]
    accumulate(slots, held, total, 1, 0, x * (RB_DEV // NX), RB_DEV, tiles, ((1,), (0,)))
    for k, out in enumerate((o0, o1, o2, o3)):
        out[...] = total[k * ROWS_OWN : (k + 1) * ROWS_OWN, :]


def backward_kernel(
    pos, slots, tiles, p0, p1, p2, p3, carried, o0, o1, far_a, far_b, o3, held, total
):
    y, x = pos[0], pos[2]
    for j, piece in enumerate((p0, p1, p2, p3)):
        from_x = lax.rem(x + (NX - j), NX)
        held[pl.ds(pl.multiple_of(from_x * ROWS_OWN, 256), ROWS_OWN), :] = piece[...]
    accumulate(slots, held, total, 0, 1, y * (CB_DEV // NY), CB_DEV, tiles, ((0,), (0,)))
    big, half = o0.shape[0], o0.shape[0] // 2
    o0[...] = total[0:big, :]
    o1[...] = total[big : 2 * big, :]
    o3[...] = total[3 * big :, :]
    for out, start in ((far_a, 2 * big), (far_b, 2 * big + half)):
        out[0:half, :] = total[start : start + half, :]
        out[half:, :] = carried[...]


def pair_kernel(up, own, down, low, high):
    low[0:COLS_OWN, :] = up[...]
    low[COLS_OWN:, :] = own[...]
    high[0:COLS_OWN, :] = own[...]
    high[COLS_OWN:, :] = down[...]


def join_kernel(*refs):
    *pieces, carried, line, passed = refs
    passed[...] = carried[...]
    start = 0
    for piece in pieces:
        line[start : start + piece.shape[0], :] = piece[...]
        start += piece.shape[0]


def fan_kernel(up, own, down, three, two):
    three[0:COLS_OWN, :] = up[...]
    three[COLS_OWN : 2 * COLS_OWN, :] = own[...]
    three[2 * COLS_OWN :, :] = down[...]
    two[0:COLS_OWN, :] = up[...]
    two[COLS_OWN:, :] = own[...]


def cut_kernel(before, after, parts, first, last, copies):
    size = first.shape[0]
    first[...] = before[0:size, :]
    last[...] = after[size:, :]
    total = parts[0]
    for k in range(1, parts.shape[0]):
        total = total + parts[k]
    for k in range(copies.shape[0]):
        copies[k] = total


def relay_y_kernel(near, far_a, back, far_b, own_part, far_part, to_near, to_back, copies):
    size = near.shape[0] // 2
    to_near[0:size, :] = near[0:size, :] + far_a[0:size, :]
    to_near[size:, :] = near[size:, :]
    to_back[0:size, :] = back[0:size, :]
    to_back[size:, :] = back[size:, :] + far_b[0:size, :]
    total = (own_part[...] + far_part[...]) + (far_a[size:, :] + far_b[size:, :])
    for k in range(copies.shape[0]):
        copies[k] = total


def split_z_kernel(pos, own, before, after, carried, up, down, mine, near, back, passed):
    passed[...] = carried[...]
    z = pos[1]

    def piece(shift):
        place = pl.ds(pl.multiple_of(lax.rem(z + shift, NZ) * COLS_OWN, 32), COLS_OWN)
        return own[place, :] + (before[place, :] + after[place, :])

    for k, shift in enumerate((2, 3, 4)):
        up[k * COLS_OWN : (k + 1) * COLS_OWN, :] = piece(shift)
    for k, shift in enumerate((5, 6)):
        down[k * COLS_OWN : (k + 1) * COLS_OWN, :] = piece(shift)
    mine[...] = piece(0)
    near[...] = piece(1)
    back[...] = piece(NZ - 1)


def relay_z_kernel(mine, near, back, up, down, before, to_mine, to_near, to_back):
    to_back[...] = back[...] + up[0:COLS_OWN, :]
    to_mine[...] = mine[...] + (up[COLS_OWN : 2 * COLS_OWN, :] + down[0:COLS_OWN, :])
    to_near[...] = near[...] + (up[2 * COLS_OWN :, :] + down[COLS_OWN:, :])


def sum_kernel(a, b, c, d, before, out):
    out[...] = (a[...] + c[...]) + (b[...] + d[...])


def sum_three_kernel(a, b, c, out):
    out[...] = a[...] + (b[...] + c[...])


def halves(pos, own, other):
    first = pos[3] == 0
    a, b = own[...], other[...]
    return jnp.where(first, a, b), jnp.where(first, b, a)


def gram_kernel(pos, own, other, gram):
    left, right = halves(pos, own, other)
    mine = own[...]
    gram[0:HALF, :] = dot_tn(left, mine)
    gram[HALF:, :] = dot_tn(right, mine)


def applied(pos, own, other, inv):
    left, right = halves(pos, own, other)
    dims = ((1,), (1,))
    new_left = product_of(left, inv[0:HALF, 0:HALF], dims)
    new_right = product_of(left, inv[HALF:, 0:HALF], dims) + product_of(
        right, inv[HALF:, HALF:], dims
    )
    return new_left, new_right


def apply_gram_kernel(pos, own, other, inv, out, out_other, gram):
    new_left, new_right = applied(pos, own, other, inv)
    first = pos[3] == 0
    mine = jnp.where(first, new_left, new_right)
    out[...] = mine
    out_other[...] = jnp.where(first, new_right, new_left)
    gram[0:HALF, :] = dot_tn(new_left, mine)
    gram[HALF:, :] = dot_tn(new_right, mine)


def make_apply_scaled(scale):
    def apply_scaled_kernel(pos, own, other, inv, out):
        new_left, new_right = applied(pos, own, other, inv)
        out[...] = jnp.where(pos[3] == 0, new_left, new_right) * F32(scale)

    return apply_scaled_kernel


WIDE = 16


def thirds(x):
    high = x.astype(BF16).astype(F32)
    rest = x - high
    middle = rest.astype(BF16).astype(F32)
    return high, middle, rest - middle


def inverse_factor(matrix):
    size = matrix.shape[0]
    lane = lax.broadcasted_iota(jnp.int32, (WIDE, size), 1)
    sub = lax.broadcasted_iota(jnp.int32, (WIDE, size), 0)
    all_lanes = lax.broadcasted_iota(jnp.int32, (size, size), 1)

    def spread(column):
        return jnp.broadcast_to(column, (WIDE, size))

    def body(step, array):
        rest = size - WIDE * step
        top = array[0:WIDE, :]
        cols = [spread(top[:, j : j + 1]) for j in range(WIDE)]
        upper = jnp.zeros((WIDE, size), F32)
        for j in range(WIDE):
            root = lax.rsqrt(spread(cols[j][j : j + 1, :]))
            line = jnp.where(lane == j, root, spread(top[j : j + 1, :]) * root)
            factor = jnp.where(sub > j, cols[j] * root, 0.0)
            for later in range(j + 1, WIDE):
                entry = spread(cols[later][j : j + 1, :]) * root
                cols[later] = cols[later] - factor * entry
            top = jnp.where((lane == j) & (sub > j), 0.0, top) - factor * line
            upper = jnp.where(sub == j, line, upper)
        done = jnp.where((lane > sub) & (lane < rest), 0.0, upper)
        a, b, c = thirds(jnp.where((lane >= WIDE) & (lane < rest), upper, 0.0))
        p, q, r = thirds(jnp.where((lane < WIDE) & (lane > sub), 0.0, upper))
        left = jnp.concatenate([a, a, b, a, b, c], axis=0).astype(BF16)
        right = jnp.concatenate([p, q, p, r, q, p], axis=0).astype(BF16)
        change = lax.dot_general(
            left, right, (((0,), (0,)), ((), ())), preferred_element_type=F32
        )
        array = jnp.where(all_lanes < WIDE, 0.0, array) - change
        return pltpu.roll(jnp.concatenate([array[WIDE:], done], axis=0), size - WIDE, 1)

    return lax.fori_loop(0, size // WIDE, body, matrix)


def factor_kernel(pos, own, other, inv):
    first = pos[3] == 0
    a, b = own[...], other[...]
    left = jnp.where(first, a, b)
    corner = jnp.where(first, b, a)[HALF:, :]
    inv_first = inverse_factor(left[0:HALF, :])
    below = left[HALF:, :]
    low = dot_nt(below, inv_first)
    inv_last = inverse_factor(corner - dot_nt(low, low))
    inv[0:HALF, 0:HALF] = inv_first
    inv[0:HALF, HALF:] = jnp.zeros((HALF, HALF), F32)
    inv[HALF:, 0:HALF] = -dot_nn(inv_last, dot_nn(low, inv_first))
    inv[HALF:, HALF:] = inv_last


def call(kernel, shapes, scalars, arrays, scratch=(), before=()):
    smem = pl.BlockSpec(memory_space=pltpu.SMEM)
    vmem = pl.BlockSpec(memory_space=pltpu.VMEM)
    anywhere = pl.BlockSpec(memory_space=pl.ANY)
    return pl.pallas_call(
        kernel,
        out_shape=[jax.ShapeDtypeStruct(shape, F32) for shape in shapes],
        in_specs=[smem] * len(scalars) + [vmem] * len(arrays) + [anywhere] * len(before),
        out_specs=[vmem] * len(shapes),
        scratch_shapes=[pltpu.VMEM(shape, F32) for shape in scratch],
        compiler_params=pltpu.CompilerParams(vmem_limit_bytes=VMEM_LIMIT),
        cost_estimate=pl.CostEstimate(flops=1000000, bytes_accessed=100000, transcendentals=0),
    )(*scalars, *arrays, *before)


def ring(size, shift):
    return [(i, (i + shift) % size) for i in range(size)]


def send(value, axis, shift):
    size = {"y": NY, "z": NZ, "col": NX, "rep": 2}[axis]
    return lax.ppermute(value, axis, ring(size, shift))


def shards(tiles, block_row, block_col, live_rows, omega):
    local_tiles = tiles[0, 0]
    slots = jnp.concatenate([block_row[0], block_col[0], live_rows[0]], axis=0)
    pos = jnp.stack([lax.axis_index(a) for a in ("y", "z", "col", "rep")]).astype(jnp.int32)
    big = CB_DEV // NY * BS
    grams = (2 * HALF, HALF)
    chunks = (NZ, 2 * HALF // NZ, HALF)

    def sum_ring(value, axis, before=pos):
        got = [value] + [send(value, axis, k) for k in range(1, 4)]
        return call(sum_kernel, [value.shape], [], got, (), [before])[0]

    def exchange_z(parts):
        return lax.all_to_all(parts, "z", 0, 0)

    def gather_panel(own, gram=None):
        carried = own[0:8] if gram is None else sum_ring(sum_ring(gram, "y"), "col")
        up, down = send(own, "z", 1), send(own, "z", NZ - 1)
        if gram is None:
            far = send(own, "z", 4)
            low, high = call(pair_kernel, [(2 * COLS_OWN, HALF)] * 2, [], [up, own, down])
            line = [far, send(low, "z", 2), up, own, down, send(high, "z", NZ - 2)]
        else:
            three, two = call(
                fan_kernel, [(3 * COLS_OWN, HALF), (2 * COLS_OWN, HALF)], [], [up, own, down]
            )
            line = [send(three, "z", 3), up, own, down, send(two, "z", NZ - 3)]
        line, carried = call(
            join_kernel, [(big, HALF), carried.shape], [], [*line, carried]
        )
        before, after = send(line, "y", 1), send(line, "y", NY - 1)
        if gram is None:
            parts = carried.reshape(1, *carried.shape)
        else:
            parts = exchange_z(carried.reshape(chunks))
        first, last, copies = call(
            cut_kernel, [(big // 2, HALF)] * 2 + [parts.shape], [], [before, after, parts]
        )
        far_a, far_b = send(first, "y", 1), send(last, "y", NY - 1)
        if gram is None:
            return [line, before, after, far_a, far_b], carried
        return [line, before, after, far_a, far_b], exchange_z(copies).reshape(grams)

    def gather_rows(own):
        return [own] + [send(own, "col", k) for k in range(1, NX)]

    def forward(pieces, carried):
        *out, passed = call(
            forward_kernel,
            [(ROWS_OWN, HALF)] * NX + [carried.shape],
            [pos, slots],
            [local_tiles, *pieces, carried],
            [(CB_DEV * BS, HALF), (RB_DEV * BS, HALF)],
        )
        return [out[0]] + [send(out[k], "col", k) for k in range(1, NX)], passed

    def forward_sum(got, before):
        return call(sum_kernel, [(ROWS_OWN, HALF)], [], got, (), [before])[0]

    def backward(pieces, gram):
        part = sum_ring(jnp.sum(exchange_z(gram.reshape(chunks)), axis=0), "col")
        far = (big // 2 + part.shape[0], HALF)
        far_part = send(part, "y", 2)
        own, near, far_a, far_b, back = call(
            backward_kernel,
            [(big, HALF)] * 2 + [far] * 2 + [(big, HALF)],
            [pos, slots],
            [local_tiles, *pieces, part],
            [(RB_DEV * BS, HALF), (CB_DEV * BS, HALF)],
        )
        far_a, far_b = send(far_a, "y", 1), send(far_b, "y", NY - 1)
        near, back, copies = call(
            relay_y_kernel,
            [(big, HALF)] * 2 + [chunks],
            [],
            [near, far_a, back, far_b, part, far_part],
        )
        before, after = send(near, "y", 1), send(back, "y", NY - 1)
        mine = exchange_z(copies).reshape(grams)
        other = send(mine, "rep", 1)
        piece = (COLS_OWN, HALF)
        up, down, own, near, back, other = call(
            split_z_kernel,
            [(3 * COLS_OWN, HALF), (2 * COLS_OWN, HALF), piece, piece, piece, grams],
            [pos],
            [own, before, after, other],
        )
        up, down = send(up, "z", 3), send(down, "z", NZ - 3)
        inv = factor(mine, other)
        own, near, back = call(
            relay_z_kernel, [piece] * 3, [], [own, near, back, up, down], (), [inv]
        )
        got = [own, send(near, "z", 1), send(back, "z", NZ - 1)]
        return call(sum_three_kernel, [piece], [], got)[0], inv

    def sum_gram(gram):
        count, chunk = NY * NX, 2 * HALF // (NY * NX)
        parts = lax.all_to_all(gram.reshape(count, chunk, HALF), ("y", "col"), 0, 0)
        part = jnp.sum(parts, axis=0)
        parts = lax.all_to_all(jnp.broadcast_to(part[None], (NZ, chunk, HALF)), "z", 0, 0)
        part = jnp.sum(parts, axis=0)
        whole = lax.all_to_all(
            jnp.broadcast_to(part[None], (count, chunk, HALF)), ("y", "col"), 0, 0
        )
        return whole.reshape(grams)

    def factor(mine, other):
        return call(factor_kernel, [(2 * HALF, 2 * HALF)], [pos], [mine, other])[0]

    def normalised(value, inv):
        other = send(value, "rep", 1)
        shape = value.shape
        return call(apply_gram_kernel, [shape, shape, grams], [pos], [value, other, inv])

    def finished(value, other, inv, scale):
        return call(make_apply_scaled(scale), [value.shape], [pos], [value, other, inv])[0]

    got, _ = forward(*gather_panel(omega[0]))
    own = forward_sum(got, pos)
    gram = call(gram_kernel, [grams], [pos], [own, send(own, "rep", 1)])[0]
    total_rows = ROWS_OWN * NX * NY * NZ
    total_cols = COLS_OWN * NX * NY * NZ
    for step in range(ITERS):
        value, inv = backward(gather_rows(own), gram)
        panel, panel_other, gram = normalised(value, inv)
        pieces, mine = gather_panel(panel, gram)
        got, other = forward(pieces, send(mine, "rep", 1))
        inv = factor(mine, other)
        if step == ITERS - 1:
            panel_basis = finished(panel, panel_other, inv, math.sqrt(total_cols))
        own, other, gram = normalised(
            forward_sum(got, panel_basis if step == ITERS - 1 else inv), inv
        )
    mine = sum_gram(gram)
    inv = factor(mine, send(mine, "rep", 1))
    basis = finished(own, other, inv, math.sqrt(total_rows))
    return basis[None], panel_basis[None]


def solution(mesh):
    fine = Mesh(mesh.devices.reshape(NY, NZ, NX, 2), ("y", "z", "col", "rep"))
    row = ("y", "z")
    placed = (
        P(row, "col", None, None, None),
        P(row, "col", None),
        P(row, "col", None),
        P(row, "col", None),
        P("col", row, "rep"),
    )
    return jax.shard_map(
        shards,
        mesh=fine,
        in_specs=placed,
        out_specs=(P(row, "col", "rep"), P("col", row, "rep")),
        check_vma=False,
    )
```

```python
import math

import jax
import jax.numpy as jnp
from jax import lax
from jax.experimental import pallas as pl
from jax.experimental.pallas import tpu as pltpu
from jax.sharding import Mesh
from jax.sharding import PartitionSpec as P

ITERS = 2
RB_DEV = 24
CB_DEV = 40
BS = 128
HALF = 128
NY = 4
NZ = 8
NX = 4
ROWS_OWN = 768
COLS_OWN = 160
UNROLL = 8
F32 = jnp.float32
BF16 = jnp.bfloat16
VMEM_LIMIT = 16 * 1024 * 1024


def dot_nn(a, b):
    return lax.dot_general(
        a, b, (((1,), (0,)), ((), ())), precision=lax.Precision.HIGHEST, preferred_element_type=F32
    )


def dot_nt(a, b):
    return lax.dot_general(
        a, b, (((1,), (1,)), ((), ())), precision=lax.Precision.HIGHEST, preferred_element_type=F32
    )


def dot_tn(a, b):
    return lax.dot_general(
        a, b, (((0,), (0,)), ((), ())), precision=lax.Precision.HIGHEST, preferred_element_type=F32
    )


def split(x):
    high = x.astype(BF16)
    return high, (x - high.astype(F32)).astype(BF16)


def product_of(a, b, dims):
    (axis_a,), (axis_b,) = dims
    pair = jnp.concatenate(split(b), axis=1 - axis_b)
    both = lax.dot_general(
        jnp.concatenate(split(a), axis=axis_a),
        jnp.concatenate([pair, pair], axis=axis_b),
        (dims, ((), ())),
        preferred_element_type=F32,
    )
    return both[:, :HALF] + both[:, HALF:]


def masked_tile(tiles, slots, slot):
    iota = lax.broadcasted_iota(jnp.int32, (BS, BS), 0)
    return jnp.where(iota < slots[2, slot], tiles[slot], F32(0.0))


def block_at(index):
    return pl.ds(pl.multiple_of(index * BS, BS), BS)


def accumulate(slots, held, total, source, target, shift, count, tiles, dims):
    def body(step, carry):
        base = step * UNROLL
        products = []
        for offset in range(UNROLL):
            slot = base + offset
            tile = masked_tile(tiles, slots, slot)
            products.append(product_of(tile, held[block_at(slots[source, slot]), :], dims))
        for offset in range(UNROLL):
            place = lax.rem(slots[target, base + offset] + (count - shift), count)
            total[block_at(place), :] += products[offset]
        return carry

    total[...] = jnp.zeros_like(total)
    lax.fori_loop(0, tiles.shape[0] // UNROLL, body, 0)


def forward_kernel(
    pos, slots, tiles, line, before, after, far_a, far_b, carried, o0, o1, o2, o3, passed, held, total
):
    y, z, x = pos[0], pos[1], pos[2]
    passed[...] = carried[...]
    half = NZ // 2
    parts = [(0, line, 0), (NY - 1, before, 0), (1, after, 0), (2, far_a, 0), (2, far_b, half)]
    for shift, ref, first in parts:
        from_y = lax.rem(y + shift, NY)
        for k in range(ref.shape[0] // COLS_OWN):
            from_z = lax.rem(z + (half + first + k), NZ)
            place = pl.multiple_of((from_y * NZ + from_z) * COLS_OWN, 32)
            held[pl.ds(place, COLS_OWN), :] = ref[k * COLS_OWN : (k + 1) * COLS_OWN, :]
    accumulate(slots, held, total, 1, 0, x * (RB_DEV // NX), RB_DEV, tiles, ((1,), (0,)))
    for k, out in enumerate((o0, o1, o2, o3)):
        out[...] = total[k * ROWS_OWN : (k + 1) * ROWS_OWN, :]


def backward_kernel(
    pos, slots, tiles, p0, p1, p2, p3, carried, o0, o1, far_a, far_b, o3, held, total
):
    y, x = pos[0], pos[2]
    for j, piece in enumerate((p0, p1, p2, p3)):
        from_x = lax.rem(x + (NX - j), NX)
        held[pl.ds(pl.multiple_of(from_x * ROWS_OWN, 256), ROWS_OWN), :] = piece[...]
    accumulate(slots, held, total, 0, 1, y * (CB_DEV // NY), CB_DEV, tiles, ((0,), (0,)))
    big, half = o0.shape[0], o0.shape[0] // 2
    o0[...] = total[0:big, :]
    o1[...] = total[big : 2 * big, :]
    o3[...] = total[3 * big :, :]
    for out, start in ((far_a, 2 * big), (far_b, 2 * big + half)):
        out[0:half, :] = total[start : start + half, :]
        out[half:, :] = carried[...]


def pair_kernel(up, own, down, low, high):
    low[0:COLS_OWN, :] = up[...]
    low[COLS_OWN:, :] = own[...]
    high[0:COLS_OWN, :] = own[...]
    high[COLS_OWN:, :] = down[...]


def fan_kernel(up, own, down, parts, three, two, total):
    three[0:COLS_OWN, :] = up[...]
    three[COLS_OWN : 2 * COLS_OWN, :] = own[...]
    three[2 * COLS_OWN :, :] = down[...]
    two[0:COLS_OWN, :] = up[...]
    two[COLS_OWN:, :] = own[...]
    value = parts[0]
    for k in range(1, parts.shape[0]):
        value = value + parts[k]
    total[...] = value


def join_kernel(*refs):
    *pieces, line = refs
    start = 0
    for piece in pieces:
        line[start : start + piece.shape[0], :] = piece[...]
        start += piece.shape[0]


def join_copies_kernel(a, b, c, d, *refs):
    *pieces, line, copies = refs
    join_kernel(*pieces, line)
    total = (a[...] + c[...]) + (b[...] + d[...])
    for k in range(copies.shape[0]):
        copies[k] = total


def cut_kernel(after_that, back, before, first, last):
    size = first.shape[0]
    first[...] = after_that[0:size, :]
    last[...] = back[size:, :]


def relay_y_kernel(near, far_a, back, far_b, own_part, far_part, to_near, to_back, copies):
    size = near.shape[0] // 2
    to_near[0:size, :] = near[0:size, :] + far_a[0:size, :]
    to_near[size:, :] = near[size:, :]
    to_back[0:size, :] = back[0:size, :]
    to_back[size:, :] = back[size:, :] + far_b[0:size, :]
    total = (own_part[...] + far_part[...]) + (far_a[size:, :] + far_b[size:, :])
    for k in range(copies.shape[0]):
        copies[k] = total


def split_z_kernel(pos, own, before, after, carried, up, down, mine, near, back, passed):
    passed[...] = carried[...]
    z = pos[1]

    def piece(shift):
        place = pl.ds(pl.multiple_of(lax.rem(z + shift, NZ) * COLS_OWN, 32), COLS_OWN)
        return own[place, :] + (before[place, :] + after[place, :])

    for k, shift in enumerate((2, 3, 4)):
        up[k * COLS_OWN : (k + 1) * COLS_OWN, :] = piece(shift)
    for k, shift in enumerate((5, 6)):
        down[k * COLS_OWN : (k + 1) * COLS_OWN, :] = piece(shift)
    mine[...] = piece(0)
    near[...] = piece(1)
    back[...] = piece(NZ - 1)


def relay_z_kernel(mine, near, back, up, down, before, to_mine, to_near, to_back):
    to_back[...] = back[...] + up[0:COLS_OWN, :]
    to_mine[...] = mine[...] + (up[COLS_OWN : 2 * COLS_OWN, :] + down[0:COLS_OWN, :])
    to_near[...] = near[...] + (up[2 * COLS_OWN :, :] + down[COLS_OWN:, :])


def sum_kernel(a, b, c, d, before, out):
    out[...] = (a[...] + c[...]) + (b[...] + d[...])


def sum_three_kernel(a, b, c, out):
    out[...] = a[...] + (b[...] + c[...])


def halves(pos, own, other):
    first = pos[3] == 0
    a, b = own[...], other[...]
    return jnp.where(first, a, b), jnp.where(first, b, a)


def gram_kernel(pos, own, other, gram):
    left, right = halves(pos, own, other)
    mine = own[...]
    gram[0:HALF, :] = dot_tn(left, mine)
    gram[HALF:, :] = dot_tn(right, mine)


def applied(pos, own, other, inv):
    left, right = halves(pos, own, other)
    dims = ((1,), (1,))
    new_left = product_of(left, inv[0:HALF, 0:HALF], dims)
    new_right = product_of(left, inv[HALF:, 0:HALF], dims) + product_of(
        right, inv[HALF:, HALF:], dims
    )
    return new_left, new_right


def apply_gram_kernel(pos, own, other, inv, out, out_other, gram):
    new_left, new_right = applied(pos, own, other, inv)
    first = pos[3] == 0
    mine = jnp.where(first, new_left, new_right)
    out[...] = mine
    out_other[...] = jnp.where(first, new_right, new_left)
    gram[0:HALF, :] = dot_tn(new_left, mine)
    gram[HALF:, :] = dot_tn(new_right, mine)


def make_apply_scaled(scale):
    def apply_scaled_kernel(pos, own, other, inv, out):
        new_left, new_right = applied(pos, own, other, inv)
        out[...] = jnp.where(pos[3] == 0, new_left, new_right) * F32(scale)

    return apply_scaled_kernel


WIDE = 16


def thirds(x):
    high = x.astype(BF16).astype(F32)
    rest = x - high
    middle = rest.astype(BF16).astype(F32)
    return high, middle, rest - middle


def inverse_factor(matrix):
    size = matrix.shape[0]
    lane = lax.broadcasted_iota(jnp.int32, (WIDE, size), 1)
    sub = lax.broadcasted_iota(jnp.int32, (WIDE, size), 0)
    all_lanes = lax.broadcasted_iota(jnp.int32, (size, size), 1)

    def spread(column):
        return jnp.broadcast_to(column, (WIDE, size))

    def body(step, array):
        rest = size - WIDE * step
        top = array[0:WIDE, :]
        cols = [spread(top[:, j : j + 1]) for j in range(WIDE)]
        upper = jnp.zeros((WIDE, size), F32)
        for j in range(WIDE):
            root = lax.rsqrt(spread(cols[j][j : j + 1, :]))
            line = jnp.where(lane == j, root, spread(top[j : j + 1, :]) * root)
            factor = jnp.where(sub > j, cols[j] * root, 0.0)
            for later in range(j + 1, WIDE):
                entry = spread(cols[later][j : j + 1, :]) * root
                cols[later] = cols[later] - factor * entry
            top = jnp.where((lane == j) & (sub > j), 0.0, top) - factor * line
            upper = jnp.where(sub == j, line, upper)
        done = jnp.where((lane > sub) & (lane < rest), 0.0, upper)
        a, b, c = thirds(jnp.where((lane >= WIDE) & (lane < rest), upper, 0.0))
        p, q, r = thirds(jnp.where((lane < WIDE) & (lane > sub), 0.0, upper))
        left = jnp.concatenate([a, a, b, a, b, c], axis=0).astype(BF16)
        right = jnp.concatenate([p, q, p, r, q, p], axis=0).astype(BF16)
        change = lax.dot_general(
            left, right, (((0,), (0,)), ((), ())), preferred_element_type=F32
        )
        array = jnp.where(all_lanes < WIDE, 0.0, array) - change
        return pltpu.roll(jnp.concatenate([array[WIDE:], done], axis=0), size - WIDE, 1)

    return lax.fori_loop(0, size // WIDE, body, matrix)


def factor_kernel(pos, own, other, inv):
    first = pos[3] == 0
    a, b = own[...], other[...]
    left = jnp.where(first, a, b)
    corner = jnp.where(first, b, a)[HALF:, :]
    inv_first = inverse_factor(left[0:HALF, :])
    below = left[HALF:, :]
    low = dot_nt(below, inv_first)
    inv_last = inverse_factor(corner - dot_nt(low, low))
    inv[0:HALF, 0:HALF] = inv_first
    inv[0:HALF, HALF:] = jnp.zeros((HALF, HALF), F32)
    inv[HALF:, 0:HALF] = -dot_nn(inv_last, dot_nn(low, inv_first))
    inv[HALF:, HALF:] = inv_last


def call(kernel, shapes, scalars, arrays, scratch=(), before=()):
    smem = pl.BlockSpec(memory_space=pltpu.SMEM)
    vmem = pl.BlockSpec(memory_space=pltpu.VMEM)
    anywhere = pl.BlockSpec(memory_space=pl.ANY)
    return pl.pallas_call(
        kernel,
        out_shape=[jax.ShapeDtypeStruct(shape, F32) for shape in shapes],
        in_specs=[smem] * len(scalars) + [vmem] * len(arrays) + [anywhere] * len(before),
        out_specs=[vmem] * len(shapes),
        scratch_shapes=[pltpu.VMEM(shape, F32) for shape in scratch],
        compiler_params=pltpu.CompilerParams(vmem_limit_bytes=VMEM_LIMIT),
        cost_estimate=pl.CostEstimate(flops=1000000, bytes_accessed=100000, transcendentals=0),
    )(*scalars, *arrays, *before)


def ring(size, shift):
    return [(i, (i + shift) % size) for i in range(size)]


def send(value, axis, shift):
    size = {"y": NY, "z": NZ, "col": NX, "rep": 2}[axis]
    return lax.ppermute(value, axis, ring(size, shift))


def shards(tiles, block_row, block_col, live_rows, omega):
    local_tiles = tiles[0, 0]
    slots = jnp.concatenate([block_row[0], block_col[0], live_rows[0]], axis=0)
    pos = jnp.stack([lax.axis_index(a) for a in ("y", "z", "col", "rep")]).astype(jnp.int32)
    big = CB_DEV // NY * BS
    grams = (2 * HALF, HALF)
    chunks = (NZ, 2 * HALF // NZ, HALF)

    def sum_ring(value, axis, before=pos):
        got = [value] + [send(value, axis, k) for k in range(1, 4)]
        return call(sum_kernel, [value.shape], [], got, (), [before])[0]

    def exchange_z(parts):
        return lax.all_to_all(parts, "z", 0, 0)

    def spread_y(line, done):
        before, after = send(line, "y", 1), send(line, "y", NY - 1)
        first, last = call(cut_kernel, [(big // 2, HALF)] * 2, [], [before, after], (), [done])
        return [line, before, after, send(first, "y", 1), send(last, "y", NY - 1)]

    def gather_first(own):
        up, down, far = (send(own, "z", k) for k in (1, NZ - 1, 4))
        low, high = call(pair_kernel, [(2 * COLS_OWN, HALF)] * 2, [], [up, own, down])
        line = [far, send(low, "z", 2), up, own, down, send(high, "z", NZ - 2)]
        return spread_y(call(join_kernel, [(big, HALF)], [], line)[0], pos)

    def gather_panel(own, gram):
        up, down = send(own, "z", 1), send(own, "z", NZ - 1)
        parts = exchange_z(gram.reshape(chunks))
        three, two, part = call(
            fan_kernel,
            [(3 * COLS_OWN, HALF), (2 * COLS_OWN, HALF), chunks[1:]],
            [],
            [up, own, down, parts],
        )
        line = [send(three, "z", 3), up, own, down, send(two, "z", NZ - 3)]
        part = sum_ring(part, "y")
        parts = [part] + [send(part, "col", k) for k in range(1, NX)]
        line, copies = call(join_copies_kernel, [(big, HALF), chunks], [], [*parts, *line])
        whole = exchange_z(copies).reshape(grams)
        return spread_y(line, whole), whole

    def gather_rows(own):
        return [own] + [send(own, "col", k) for k in range(1, NX)]

    def forward(pieces, carried):
        *out, passed = call(
            forward_kernel,
            [(ROWS_OWN, HALF)] * NX + [carried.shape],
            [pos, slots],
            [local_tiles, *pieces, carried],
            [(CB_DEV * BS, HALF), (RB_DEV * BS, HALF)],
        )
        return [out[0]] + [send(out[k], "col", k) for k in range(1, NX)], passed

    def forward_sum(got, before):
        return call(sum_kernel, [(ROWS_OWN, HALF)], [], got, (), [before])[0]

    def backward(pieces, gram):
        part = sum_ring(jnp.sum(exchange_z(gram.reshape(chunks)), axis=0), "col")
        far = (big // 2 + part.shape[0], HALF)
        far_part = send(part, "y", 2)
        own, near, far_a, far_b, back = call(
            backward_kernel,
            [(big, HALF)] * 2 + [far] * 2 + [(big, HALF)],
            [pos, slots],
            [local_tiles, *pieces, part],
            [(RB_DEV * BS, HALF), (CB_DEV * BS, HALF)],
        )
        far_a, far_b = send(far_a, "y", 1), send(far_b, "y", NY - 1)
        near, back, copies = call(
            relay_y_kernel,
            [(big, HALF)] * 2 + [chunks],
            [],
            [near, far_a, back, far_b, part, far_part],
        )
        before, after = send(near, "y", 1), send(back, "y", NY - 1)
        mine = exchange_z(copies).reshape(grams)
        other = send(mine, "rep", 1)
        piece = (COLS_OWN, HALF)
        up, down, own, near, back, other = call(
            split_z_kernel,
            [(3 * COLS_OWN, HALF), (2 * COLS_OWN, HALF), piece, piece, piece, grams],
            [pos],
            [own, before, after, other],
        )
        up, down = send(up, "z", 3), send(down, "z", NZ - 3)
        inv = factor(mine, other)
        own, near, back = call(
            relay_z_kernel, [piece] * 3, [], [own, near, back, up, down], (), [inv]
        )
        got = [own, send(near, "z", 1), send(back, "z", NZ - 1)]
        return call(sum_three_kernel, [piece], [], got)[0], inv

    def sum_gram(gram):
        count, chunk = NY * NX, 2 * HALF // (NY * NX)
        parts = lax.all_to_all(gram.reshape(count, chunk, HALF), ("y", "col"), 0, 0)
        part = jnp.sum(parts, axis=0)
        parts = lax.all_to_all(jnp.broadcast_to(part[None], (NZ, chunk, HALF)), "z", 0, 0)
        part = jnp.sum(parts, axis=0)
        whole = lax.all_to_all(
            jnp.broadcast_to(part[None], (count, chunk, HALF)), ("y", "col"), 0, 0
        )
        return whole.reshape(grams)

    def factor(mine, other):
        return call(factor_kernel, [(2 * HALF, 2 * HALF)], [pos], [mine, other])[0]

    def normalised(value, inv):
        other = send(value, "rep", 1)
        shape = value.shape
        return call(apply_gram_kernel, [shape, shape, grams], [pos], [value, other, inv])

    def finished(value, other, inv, scale):
        return call(make_apply_scaled(scale), [value.shape], [pos], [value, other, inv])[0]

    got, _ = forward(gather_first(omega[0]), omega[0, 0:8])
    own = forward_sum(got, pos)
    gram = call(gram_kernel, [grams], [pos], [own, send(own, "rep", 1)])[0]
    total_rows = ROWS_OWN * NX * NY * NZ
    total_cols = COLS_OWN * NX * NY * NZ
    for step in range(ITERS):
        value, inv = backward(gather_rows(own), gram)
        panel, panel_other, gram = normalised(value, inv)
        pieces, mine = gather_panel(panel, gram)
        got, other = forward(pieces, send(mine, "rep", 1))
        inv = factor(mine, other)
        if step == ITERS - 1:
            panel_basis = finished(panel, panel_other, inv, math.sqrt(total_cols))
        own, other, gram = normalised(
            forward_sum(got, panel_basis if step == ITERS - 1 else inv), inv
        )
    mine = sum_gram(gram)
    inv = factor(mine, send(mine, "rep", 1))
    basis = finished(own, other, inv, math.sqrt(total_rows))
    return basis[None], panel_basis[None]


def solution(mesh):
    fine = Mesh(mesh.devices.reshape(NY, NZ, NX, 2), ("y", "z", "col", "rep"))
    row = ("y", "z")
    placed = (
        P(row, "col", None, None, None),
        P(row, "col", None),
        P(row, "col", None),
        P(row, "col", None),
        P("col", row, "rep"),
    )
    return jax.shard_map(
        shards,
        mesh=fine,
        in_specs=placed,
        out_specs=(P(row, "col", "rep"), P("col", row, "rep")),
        check_vma=False,
    )
```

```python
import math

import jax
import jax.numpy as jnp
from jax import lax
from jax.experimental import pallas as pl
from jax.experimental.pallas import tpu as pltpu
from jax.sharding import Mesh
from jax.sharding import PartitionSpec as P

ITERS = 2
RB_DEV = 24
CB_DEV = 40
BS = 128
HALF = 128
NY = 4
NZ = 8
NX = 4
ROWS_OWN = 768
COLS_OWN = 160
UNROLL = 8
F32 = jnp.float32
BF16 = jnp.bfloat16
VMEM_LIMIT = 16 * 1024 * 1024


def dot_nn(a, b):
    return lax.dot_general(
        a, b, (((1,), (0,)), ((), ())), precision=lax.Precision.HIGHEST, preferred_element_type=F32
    )


def dot_nt(a, b):
    return lax.dot_general(
        a, b, (((1,), (1,)), ((), ())), precision=lax.Precision.HIGHEST, preferred_element_type=F32
    )


def dot_tn(a, b):
    return lax.dot_general(
        a, b, (((0,), (0,)), ((), ())), precision=lax.Precision.HIGHEST, preferred_element_type=F32
    )


def split(x):
    high = x.astype(BF16)
    return high, (x - high.astype(F32)).astype(BF16)


def product_of(a, b, dims):
    (axis_a,), (axis_b,) = dims
    pair = jnp.concatenate(split(b), axis=1 - axis_b)
    both = lax.dot_general(
        jnp.concatenate(split(a), axis=axis_a),
        jnp.concatenate([pair, pair], axis=axis_b),
        (dims, ((), ())),
        preferred_element_type=F32,
    )
    return both[:, :HALF] + both[:, HALF:]


def masked_tile(tiles, slots, slot):
    iota = lax.broadcasted_iota(jnp.int32, (BS, BS), 0)
    return jnp.where(iota < slots[2, slot], tiles[slot], F32(0.0))


def block_at(index):
    return pl.ds(pl.multiple_of(index * BS, BS), BS)


def accumulate(slots, held, total, source, target, shift, count, tiles, dims):
    def body(step, carry):
        base = step * UNROLL
        products = []
        for offset in range(UNROLL):
            slot = base + offset
            tile = masked_tile(tiles, slots, slot)
            products.append(product_of(tile, held[block_at(slots[source, slot]), :], dims))
        for offset in range(UNROLL):
            place = lax.rem(slots[target, base + offset] + (count - shift), count)
            total[block_at(place), :] += products[offset]
        return carry

    total[...] = jnp.zeros_like(total)
    lax.fori_loop(0, tiles.shape[0] // UNROLL, body, 0)


def forward_kernel(
    pos, slots, tiles, line, before, after, far_a, far_b, carried, o0, o1, o2, o3, passed, held, total
):
    y, z, x = pos[0], pos[1], pos[2]
    passed[...] = carried[...]
    half = NZ // 2
    parts = [(0, line, 0), (NY - 1, before, 0), (1, after, 0), (2, far_a, 0), (2, far_b, half)]
    for shift, ref, first in parts:
        from_y = lax.rem(y + shift, NY)
        for k in range(ref.shape[0] // COLS_OWN):
            from_z = lax.rem(z + (half + first + k), NZ)
            place = pl.multiple_of((from_y * NZ + from_z) * COLS_OWN, 32)
            held[pl.ds(place, COLS_OWN), :] = ref[k * COLS_OWN : (k + 1) * COLS_OWN, :]
    accumulate(slots, held, total, 1, 0, x * (RB_DEV // NX), RB_DEV, tiles, ((1,), (0,)))
    for k, out in enumerate((o0, o1, o2, o3)):
        out[...] = total[k * ROWS_OWN : (k + 1) * ROWS_OWN, :]


def backward_kernel(
    pos, slots, tiles, p0, p1, p2, p3, carried, o0, o1, far_a, far_b, o3, held, total
):
    y, x = pos[0], pos[2]
    for j, piece in enumerate((p0, p1, p2, p3)):
        from_x = lax.rem(x + (NX - j), NX)
        held[pl.ds(pl.multiple_of(from_x * ROWS_OWN, 256), ROWS_OWN), :] = piece[...]
    accumulate(slots, held, total, 0, 1, y * (CB_DEV // NY), CB_DEV, tiles, ((0,), (0,)))
    big, half = o0.shape[0], o0.shape[0] // 2
    o0[...] = total[0:big, :]
    o1[...] = total[big : 2 * big, :]
    o3[...] = total[3 * big :, :]
    for out, start in ((far_a, 2 * big), (far_b, 2 * big + half)):
        out[0:half, :] = total[start : start + half, :]
        out[half:, :] = carried[...]


def pair_kernel(up, own, down, low, high):
    low[0:COLS_OWN, :] = up[...]
    low[COLS_OWN:, :] = own[...]
    high[0:COLS_OWN, :] = own[...]
    high[COLS_OWN:, :] = down[...]


def fan_kernel(up, own, down, parts, low, high, total):
    pair_kernel(up, own, down, low, high)
    value = parts[0]
    for k in range(1, parts.shape[0]):
        value = value + parts[k]
    total[...] = value


def join_kernel(*refs):
    *pieces, before, line = refs
    start = 0
    for piece in pieces:
        line[start : start + piece.shape[0], :] = piece[...]
        start += piece.shape[0]


def copies_kernel(a, b, c, d, copies):
    total = (a[...] + c[...]) + (b[...] + d[...])
    for k in range(copies.shape[0]):
        copies[k] = total


def cut_kernel(after_that, back, before, first, last):
    size = first.shape[0]
    first[...] = after_that[0:size, :]
    last[...] = back[size:, :]


def relay_y_kernel(near, far_a, back, far_b, own_part, far_part, to_near, to_back, copies):
    size = near.shape[0] // 2
    to_near[0:size, :] = near[0:size, :] + far_a[0:size, :]
    to_near[size:, :] = near[size:, :]
    to_back[0:size, :] = back[0:size, :]
    to_back[size:, :] = back[size:, :] + far_b[0:size, :]
    total = (own_part[...] + far_part[...]) + (far_a[size:, :] + far_b[size:, :])
    for k in range(copies.shape[0]):
        copies[k] = total


def split_z_kernel(pos, own, before, after, carried, up, down, mine, near, back, passed):
    passed[...] = carried[...]
    z = pos[1]

    def piece(shift):
        place = pl.ds(pl.multiple_of(lax.rem(z + shift, NZ) * COLS_OWN, 32), COLS_OWN)
        return own[place, :] + (before[place, :] + after[place, :])

    for k, shift in enumerate((2, 3, 4)):
        up[k * COLS_OWN : (k + 1) * COLS_OWN, :] = piece(shift)
    for k, shift in enumerate((5, 6)):
        down[k * COLS_OWN : (k + 1) * COLS_OWN, :] = piece(shift)
    mine[...] = piece(0)
    near[...] = piece(1)
    back[...] = piece(NZ - 1)


def relay_z_kernel(mine, near, back, up, down, before, to_mine, to_near, to_back):
    to_back[...] = back[...] + up[0:COLS_OWN, :]
    to_mine[...] = mine[...] + (up[COLS_OWN : 2 * COLS_OWN, :] + down[0:COLS_OWN, :])
    to_near[...] = near[...] + (up[2 * COLS_OWN :, :] + down[COLS_OWN:, :])


def sum_kernel(a, b, c, d, before, out):
    out[...] = (a[...] + c[...]) + (b[...] + d[...])


def sum_three_kernel(a, b, c, out):
    out[...] = a[...] + (b[...] + c[...])


def halves(pos, own, other):
    first = pos[3] == 0
    a, b = own[...], other[...]
    return jnp.where(first, a, b), jnp.where(first, b, a)


def gram_kernel(pos, own, other, gram):
    left, right = halves(pos, own, other)
    mine = own[...]
    gram[0:HALF, :] = dot_tn(left, mine)
    gram[HALF:, :] = dot_tn(right, mine)


def applied(pos, own, other, inv):
    left, right = halves(pos, own, other)
    dims = ((1,), (1,))
    new_left = product_of(left, inv[0:HALF, 0:HALF], dims)
    new_right = product_of(left, inv[HALF:, 0:HALF], dims) + product_of(
        right, inv[HALF:, HALF:], dims
    )
    return new_left, new_right


def apply_gram_kernel(pos, own, other, inv, out, out_other, gram):
    new_left, new_right = applied(pos, own, other, inv)
    first = pos[3] == 0
    mine = jnp.where(first, new_left, new_right)
    out[...] = mine
    out_other[...] = jnp.where(first, new_right, new_left)
    gram[0:HALF, :] = dot_tn(new_left, mine)
    gram[HALF:, :] = dot_tn(new_right, mine)


def make_apply_scaled(scale):
    def apply_scaled_kernel(pos, own, other, inv, out):
        new_left, new_right = applied(pos, own, other, inv)
        out[...] = jnp.where(pos[3] == 0, new_left, new_right) * F32(scale)

    return apply_scaled_kernel


WIDE = 16


def thirds(x):
    high = x.astype(BF16).astype(F32)
    rest = x - high
    middle = rest.astype(BF16).astype(F32)
    return high, middle, rest - middle


def inverse_factor(matrix):
    size = matrix.shape[0]
    lane = lax.broadcasted_iota(jnp.int32, (WIDE, size), 1)
    sub = lax.broadcasted_iota(jnp.int32, (WIDE, size), 0)
    all_lanes = lax.broadcasted_iota(jnp.int32, (size, size), 1)

    def spread(column):
        return jnp.broadcast_to(column, (WIDE, size))

    def body(step, array):
        rest = size - WIDE * step
        top = array[0:WIDE, :]
        cols = [spread(top[:, j : j + 1]) for j in range(WIDE)]
        upper = jnp.zeros((WIDE, size), F32)
        for j in range(WIDE):
            root = lax.rsqrt(spread(cols[j][j : j + 1, :]))
            line = jnp.where(lane == j, root, spread(top[j : j + 1, :]) * root)
            factor = jnp.where(sub > j, cols[j] * root, 0.0)
            for later in range(j + 1, WIDE):
                entry = spread(cols[later][j : j + 1, :]) * root
                cols[later] = cols[later] - factor * entry
            top = jnp.where((lane == j) & (sub > j), 0.0, top) - factor * line
            upper = jnp.where(sub == j, line, upper)
        done = jnp.where((lane > sub) & (lane < rest), 0.0, upper)
        a, b, c = thirds(jnp.where((lane >= WIDE) & (lane < rest), upper, 0.0))
        p, q, r = thirds(jnp.where((lane < WIDE) & (lane > sub), 0.0, upper))
        left = jnp.concatenate([a, a, b, a, b, c], axis=0).astype(BF16)
        right = jnp.concatenate([p, q, p, r, q, p], axis=0).astype(BF16)
        change = lax.dot_general(
            left, right, (((0,), (0,)), ((), ())), preferred_element_type=F32
        )
        array = jnp.where(all_lanes < WIDE, 0.0, array) - change
        return pltpu.roll(jnp.concatenate([array[WIDE:], done], axis=0), size - WIDE, 1)

    return lax.fori_loop(0, size // WIDE, body, matrix)


def factor_kernel(pos, own, other, inv):
    first = pos[3] == 0
    a, b = own[...], other[...]
    left = jnp.where(first, a, b)
    corner = jnp.where(first, b, a)[HALF:, :]
    inv_first = inverse_factor(left[0:HALF, :])
    below = left[HALF:, :]
    low = dot_nt(below, inv_first)
    inv_last = inverse_factor(corner - dot_nt(low, low))
    inv[0:HALF, 0:HALF] = inv_first
    inv[0:HALF, HALF:] = jnp.zeros((HALF, HALF), F32)
    inv[HALF:, 0:HALF] = -dot_nn(inv_last, dot_nn(low, inv_first))
    inv[HALF:, HALF:] = inv_last


def call(kernel, shapes, scalars, arrays, scratch=(), before=()):
    smem = pl.BlockSpec(memory_space=pltpu.SMEM)
    vmem = pl.BlockSpec(memory_space=pltpu.VMEM)
    anywhere = pl.BlockSpec(memory_space=pl.ANY)
    return pl.pallas_call(
        kernel,
        out_shape=[jax.ShapeDtypeStruct(shape, F32) for shape in shapes],
        in_specs=[smem] * len(scalars) + [vmem] * len(arrays) + [anywhere] * len(before),
        out_specs=[vmem] * len(shapes),
        scratch_shapes=[pltpu.VMEM(shape, F32) for shape in scratch],
        compiler_params=pltpu.CompilerParams(vmem_limit_bytes=VMEM_LIMIT),
        cost_estimate=pl.CostEstimate(flops=1000000, bytes_accessed=100000, transcendentals=0),
    )(*scalars, *arrays, *before)


def ring(size, shift):
    return [(i, (i + shift) % size) for i in range(size)]


def send(value, axis, shift):
    size = {"y": NY, "z": NZ, "col": NX, "rep": 2}[axis]
    return lax.ppermute(value, axis, ring(size, shift))


def shards(tiles, block_row, block_col, live_rows, omega):
    local_tiles = tiles[0, 0]
    slots = jnp.concatenate([block_row[0], block_col[0], live_rows[0]], axis=0)
    pos = jnp.stack([lax.axis_index(a) for a in ("y", "z", "col", "rep")]).astype(jnp.int32)
    big = CB_DEV // NY * BS
    grams = (2 * HALF, HALF)
    chunks = (NZ, 2 * HALF // NZ, HALF)

    def sum_ring(value, axis, before=pos):
        got = [value] + [send(value, axis, k) for k in range(1, 4)]
        return call(sum_kernel, [value.shape], [], got, (), [before])[0]

    def exchange_z(parts):
        return lax.all_to_all(parts, "z", 0, 0)

    def spread_y(line, done):
        before, after = send(line, "y", 1), send(line, "y", NY - 1)
        first, last = call(cut_kernel, [(big // 2, HALF)] * 2, [], [before, after], (), [done])
        return [line, before, after, send(first, "y", 1), send(last, "y", NY - 1)]

    def gather_first(own):
        up, down, far = (send(own, "z", k) for k in (1, NZ - 1, 4))
        low, high = call(pair_kernel, [(2 * COLS_OWN, HALF)] * 2, [], [up, own, down])
        line = [far, send(low, "z", 2), up, own, down, send(high, "z", NZ - 2)]
        return spread_y(call(join_kernel, [(big, HALF)], [], line, (), [pos])[0], pos)

    def gather_panel(own, gram):
        up, down, far = (send(own, "z", k) for k in (1, NZ - 1, 4))
        parts = exchange_z(gram.reshape(chunks))
        low, high, part = call(
            fan_kernel, [(2 * COLS_OWN, HALF)] * 2 + [chunks[1:]], [], [up, own, down, parts]
        )
        line = [far, send(low, "z", 2), up, own, down, send(high, "z", NZ - 2)]
        part = sum_ring(part, "y")
        parts = [part] + [send(part, "col", k) for k in range(1, NX)]
        line = call(join_kernel, [(big, HALF)], [], line, (), [part])[0]
        copies = call(copies_kernel, [chunks], [], parts)[0]
        whole = exchange_z(copies).reshape(grams)
        return spread_y(line, whole), whole

    def gather_rows(own):
        return [own] + [send(own, "col", k) for k in range(1, NX)]

    def forward(pieces, carried):
        *out, passed = call(
            forward_kernel,
            [(ROWS_OWN, HALF)] * NX + [carried.shape],
            [pos, slots],
            [local_tiles, *pieces, carried],
            [(CB_DEV * BS, HALF), (RB_DEV * BS, HALF)],
        )
        return [out[0]] + [send(out[k], "col", k) for k in range(1, NX)], passed

    def forward_sum(got, before):
        return call(sum_kernel, [(ROWS_OWN, HALF)], [], got, (), [before])[0]

    def backward(pieces, gram):
        part = sum_ring(jnp.sum(exchange_z(gram.reshape(chunks)), axis=0), "col")
        far = (big // 2 + part.shape[0], HALF)
        far_part = send(part, "y", 2)
        own, near, far_a, far_b, back = call(
            backward_kernel,
            [(big, HALF)] * 2 + [far] * 2 + [(big, HALF)],
            [pos, slots],
            [local_tiles, *pieces, part],
            [(RB_DEV * BS, HALF), (CB_DEV * BS, HALF)],
        )
        far_a, far_b = send(far_a, "y", 1), send(far_b, "y", NY - 1)
        near, back, copies = call(
            relay_y_kernel,
            [(big, HALF)] * 2 + [chunks],
            [],
            [near, far_a, back, far_b, part, far_part],
        )
        before, after = send(near, "y", 1), send(back, "y", NY - 1)
        mine = exchange_z(copies).reshape(grams)
        piece = (COLS_OWN, HALF)
        up, down, own, near, back, mine = call(
            split_z_kernel,
            [(3 * COLS_OWN, HALF), (2 * COLS_OWN, HALF), piece, piece, piece, grams],
            [pos],
            [own, before, after, mine],
        )
        up, down = send(up, "z", 3), send(down, "z", NZ - 3)
        inv = factor(mine, send(mine, "rep", 1))
        own, near, back = call(
            relay_z_kernel, [piece] * 3, [], [own, near, back, up, down], (), [inv]
        )
        got = [own, send(near, "z", 1), send(back, "z", NZ - 1)]
        return call(sum_three_kernel, [piece], [], got)[0], inv

    def sum_gram(gram):
        count, chunk = NY * NX, 2 * HALF // (NY * NX)
        parts = lax.all_to_all(gram.reshape(count, chunk, HALF), ("y", "col"), 0, 0)
        part = jnp.sum(parts, axis=0)
        parts = lax.all_to_all(jnp.broadcast_to(part[None], (NZ, chunk, HALF)), "z", 0, 0)
        part = jnp.sum(parts, axis=0)
        whole = lax.all_to_all(
            jnp.broadcast_to(part[None], (count, chunk, HALF)), ("y", "col"), 0, 0
        )
        return whole.reshape(grams)

    def factor(mine, other):
        return call(factor_kernel, [(2 * HALF, 2 * HALF)], [pos], [mine, other])[0]

    def normalised(value, inv):
        other = send(value, "rep", 1)
        shape = value.shape
        return call(apply_gram_kernel, [shape, shape, grams], [pos], [value, other, inv])

    def finished(value, other, inv, scale):
        return call(make_apply_scaled(scale), [value.shape], [pos], [value, other, inv])[0]

    got, _ = forward(gather_first(omega[0]), omega[0, 0:8])
    own = forward_sum(got, pos)
    gram = call(gram_kernel, [grams], [pos], [own, send(own, "rep", 1)])[0]
    total_rows = ROWS_OWN * NX * NY * NZ
    total_cols = COLS_OWN * NX * NY * NZ
    for step in range(ITERS):
        value, inv = backward(gather_rows(own), gram)
        panel, panel_other, gram = normalised(value, inv)
        pieces, mine = gather_panel(panel, gram)
        got, other = forward(pieces, send(mine, "rep", 1))
        inv = factor(mine, other)
        if step == ITERS - 1:
            panel_basis = finished(panel, panel_other, inv, math.sqrt(total_cols))
        own, other, gram = normalised(
            forward_sum(got, panel_basis if step == ITERS - 1 else inv), inv
        )
    mine = sum_gram(gram)
    inv = factor(mine, send(mine, "rep", 1))
    basis = finished(own, other, inv, math.sqrt(total_rows))
    return basis[None], panel_basis[None]


def solution(mesh):
    fine = Mesh(mesh.devices.reshape(NY, NZ, NX, 2), ("y", "z", "col", "rep"))
    row = ("y", "z")
    placed = (
        P(row, "col", None, None, None),
        P(row, "col", None),
        P(row, "col", None),
        P(row, "col", None),
        P("col", row, "rep"),
    )
    return jax.shard_map(
        shards,
        mesh=fine,
        in_specs=placed,
        out_specs=(P(row, "col", "rep"), P("col", row, "rep")),
        check_vma=False,
    )
```

```python
import math

import jax
import jax.numpy as jnp
from jax import lax
from jax.experimental import pallas as pl
from jax.experimental.pallas import tpu as pltpu
from jax.sharding import Mesh
from jax.sharding import PartitionSpec as P

ITERS = 2
RB_DEV = 24
CB_DEV = 40
BS = 128
HALF = 128
NY = 4
NZ = 8
NX = 4
ROWS_OWN = 768
COLS_OWN = 160
UNROLL = 8
F32 = jnp.float32
BF16 = jnp.bfloat16
VMEM_LIMIT = 16 * 1024 * 1024


def dot_nn(a, b):
    return lax.dot_general(
        a, b, (((1,), (0,)), ((), ())), precision=lax.Precision.HIGHEST, preferred_element_type=F32
    )


def dot_nt(a, b):
    return lax.dot_general(
        a, b, (((1,), (1,)), ((), ())), precision=lax.Precision.HIGHEST, preferred_element_type=F32
    )


def dot_tn(a, b):
    return lax.dot_general(
        a, b, (((0,), (0,)), ((), ())), precision=lax.Precision.HIGHEST, preferred_element_type=F32
    )


def split(x):
    high = x.astype(BF16)
    return high, (x - high.astype(F32)).astype(BF16)


def product_of(a, b, dims):
    (axis_a,), (axis_b,) = dims
    pair = jnp.concatenate(split(b), axis=1 - axis_b)
    both = lax.dot_general(
        jnp.concatenate(split(a), axis=axis_a),
        jnp.concatenate([pair, pair], axis=axis_b),
        (dims, ((), ())),
        preferred_element_type=F32,
    )
    return both[:, :HALF] + both[:, HALF:]


def masked_tile(tiles, slots, slot):
    iota = lax.broadcasted_iota(jnp.int32, (BS, BS), 0)
    return jnp.where(iota < slots[2, slot], tiles[slot], F32(0.0))


def block_at(index):
    return pl.ds(pl.multiple_of(index * BS, BS), BS)


def accumulate(slots, held, total, source, target, shift, count, tiles, dims):
    def body(step, carry):
        base = step * UNROLL
        products = []
        for offset in range(UNROLL):
            slot = base + offset
            tile = masked_tile(tiles, slots, slot)
            products.append(product_of(tile, held[block_at(slots[source, slot]), :], dims))
        for offset in range(UNROLL):
            place = lax.rem(slots[target, base + offset] + (count - shift), count)
            total[block_at(place), :] += products[offset]
        return carry

    total[...] = jnp.zeros_like(total)
    lax.fori_loop(0, tiles.shape[0] // UNROLL, body, 0)


def forward_kernel(
    pos, slots, tiles, line, before, after, far_a, far_b, carried, o0, o1, o2, o3, passed, held, total
):
    y, z, x = pos[0], pos[1], pos[2]
    passed[...] = carried[...]
    half = NZ // 2
    parts = [(0, line, 0), (NY - 1, before, 0), (1, after, 0), (2, far_a, 0), (2, far_b, half)]
    for shift, ref, first in parts:
        from_y = lax.rem(y + shift, NY)
        for k in range(ref.shape[0] // COLS_OWN):
            from_z = lax.rem(z + (half + first + k), NZ)
            place = pl.multiple_of((from_y * NZ + from_z) * COLS_OWN, 32)
            held[pl.ds(place, COLS_OWN), :] = ref[k * COLS_OWN : (k + 1) * COLS_OWN, :]
    accumulate(slots, held, total, 1, 0, x * (RB_DEV // NX), RB_DEV, tiles, ((1,), (0,)))
    for k, out in enumerate((o0, o1, o2, o3)):
        out[...] = total[k * ROWS_OWN : (k + 1) * ROWS_OWN, :]


def backward_kernel(
    pos, slots, tiles, p0, p1, p2, p3, carried, o0, o1, far_a, far_b, o3, held, total
):
    y, x = pos[0], pos[2]
    for j, piece in enumerate((p0, p1, p2, p3)):
        from_x = lax.rem(x + (NX - j), NX)
        held[pl.ds(pl.multiple_of(from_x * ROWS_OWN, 256), ROWS_OWN), :] = piece[...]
    accumulate(slots, held, total, 0, 1, y * (CB_DEV // NY), CB_DEV, tiles, ((0,), (0,)))
    big, half = o0.shape[0], o0.shape[0] // 2
    o0[...] = total[0:big, :]
    o1[...] = total[big : 2 * big, :]
    o3[...] = total[3 * big :, :]
    for out, start in ((far_a, 2 * big), (far_b, 2 * big + half)):
        out[0:half, :] = total[start : start + half, :]
        out[half:, :] = carried[...]


def pair_kernel(up, own, down, low, high):
    low[0:COLS_OWN, :] = up[...]
    low[COLS_OWN:, :] = own[...]
    high[0:COLS_OWN, :] = own[...]
    high[COLS_OWN:, :] = down[...]


def fan_kernel(up, own, down, before, low, high):
    pair_kernel(up, own, down, low, high)


def sum_parts_kernel(parts, total):
    value = parts[0]
    for k in range(1, parts.shape[0]):
        value = value + parts[k]
    total[...] = value


def join_kernel(*refs):
    *pieces, before, line = refs
    start = 0
    for piece in pieces:
        line[start : start + piece.shape[0], :] = piece[...]
        start += piece.shape[0]


def copies_kernel(a, b, c, d, copies):
    total = (a[...] + c[...]) + (b[...] + d[...])
    for k in range(copies.shape[0]):
        copies[k] = total


def cut_kernel(after_that, back, before, first, last):
    size = first.shape[0]
    first[...] = after_that[0:size, :]
    last[...] = back[size:, :]


def relay_y_kernel(near, far_a, back, far_b, own_part, far_part, to_near, to_back, copies):
    size = near.shape[0] // 2
    to_near[0:size, :] = near[0:size, :] + far_a[0:size, :]
    to_near[size:, :] = near[size:, :]
    to_back[0:size, :] = back[0:size, :]
    to_back[size:, :] = back[size:, :] + far_b[0:size, :]
    total = (own_part[...] + far_part[...]) + (far_a[size:, :] + far_b[size:, :])
    for k in range(copies.shape[0]):
        copies[k] = total


def split_z_kernel(pos, own, before, after, carried, up, down, mine, near, back, passed):
    passed[...] = carried[...]
    z = pos[1]

    def piece(shift):
        place = pl.ds(pl.multiple_of(lax.rem(z + shift, NZ) * COLS_OWN, 32), COLS_OWN)
        return own[place, :] + (before[place, :] + after[place, :])

    for k, shift in enumerate((2, 3, 4)):
        up[k * COLS_OWN : (k + 1) * COLS_OWN, :] = piece(shift)
    for k, shift in enumerate((5, 6)):
        down[k * COLS_OWN : (k + 1) * COLS_OWN, :] = piece(shift)
    mine[...] = piece(0)
    near[...] = piece(1)
    back[...] = piece(NZ - 1)


def relay_z_kernel(mine, near, back, up, down, before, to_mine, to_near, to_back):
    to_back[...] = back[...] + up[0:COLS_OWN, :]
    to_mine[...] = mine[...] + (up[COLS_OWN : 2 * COLS_OWN, :] + down[0:COLS_OWN, :])
    to_near[...] = near[...] + (up[2 * COLS_OWN :, :] + down[COLS_OWN:, :])


def sum_kernel(a, b, c, d, before, out):
    out[...] = (a[...] + c[...]) + (b[...] + d[...])


def sum_three_kernel(a, b, c, out):
    out[...] = a[...] + (b[...] + c[...])


def halves(pos, own, other):
    first = pos[3] == 0
    a, b = own[...], other[...]
    return jnp.where(first, a, b), jnp.where(first, b, a)


def gram_kernel(pos, own, other, gram):
    left, right = halves(pos, own, other)
    mine = own[...]
    gram[0:HALF, :] = dot_tn(left, mine)
    gram[HALF:, :] = dot_tn(right, mine)


def applied(pos, own, other, inv):
    left, right = halves(pos, own, other)
    dims = ((1,), (1,))
    new_left = product_of(left, inv[0:HALF, 0:HALF], dims)
    new_right = product_of(left, inv[HALF:, 0:HALF], dims) + product_of(
        right, inv[HALF:, HALF:], dims
    )
    return new_left, new_right


def apply_gram_kernel(pos, own, other, inv, out, out_other, gram):
    new_left, new_right = applied(pos, own, other, inv)
    first = pos[3] == 0
    mine = jnp.where(first, new_left, new_right)
    out[...] = mine
    out_other[...] = jnp.where(first, new_right, new_left)
    gram[0:HALF, :] = dot_tn(new_left, mine)
    gram[HALF:, :] = dot_tn(new_right, mine)


def make_apply_scaled(scale):
    def apply_scaled_kernel(pos, own, other, inv, out):
        new_left, new_right = applied(pos, own, other, inv)
        out[...] = jnp.where(pos[3] == 0, new_left, new_right) * F32(scale)

    return apply_scaled_kernel


WIDE = 16


def thirds(x):
    high = x.astype(BF16).astype(F32)
    rest = x - high
    middle = rest.astype(BF16).astype(F32)
    return high, middle, rest - middle


def inverse_factor(matrix):
    size = matrix.shape[0]
    lane = lax.broadcasted_iota(jnp.int32, (WIDE, size), 1)
    sub = lax.broadcasted_iota(jnp.int32, (WIDE, size), 0)
    all_lanes = lax.broadcasted_iota(jnp.int32, (size, size), 1)

    def spread(column):
        return jnp.broadcast_to(column, (WIDE, size))

    def body(step, array):
        rest = size - WIDE * step
        top = array[0:WIDE, :]
        cols = [spread(top[:, j : j + 1]) for j in range(WIDE)]
        upper = jnp.zeros((WIDE, size), F32)
        for j in range(WIDE):
            root = lax.rsqrt(spread(cols[j][j : j + 1, :]))
            line = jnp.where(lane == j, root, spread(top[j : j + 1, :]) * root)
            factor = jnp.where(sub > j, cols[j] * root, 0.0)
            for later in range(j + 1, WIDE):
                entry = spread(cols[later][j : j + 1, :]) * root
                cols[later] = cols[later] - factor * entry
            top = jnp.where((lane == j) & (sub > j), 0.0, top) - factor * line
            upper = jnp.where(sub == j, line, upper)
        done = jnp.where((lane > sub) & (lane < rest), 0.0, upper)
        a, b, c = thirds(jnp.where((lane >= WIDE) & (lane < rest), upper, 0.0))
        p, q, r = thirds(jnp.where((lane < WIDE) & (lane > sub), 0.0, upper))
        left = jnp.concatenate([a, a, b, a, b, c], axis=0).astype(BF16)
        right = jnp.concatenate([p, q, p, r, q, p], axis=0).astype(BF16)
        change = lax.dot_general(
            left, right, (((0,), (0,)), ((), ())), preferred_element_type=F32
        )
        array = jnp.where(all_lanes < WIDE, 0.0, array) - change
        return pltpu.roll(jnp.concatenate([array[WIDE:], done], axis=0), size - WIDE, 1)

    return lax.fori_loop(0, size // WIDE, body, matrix)


def factor_kernel(pos, own, other, inv):
    first = pos[3] == 0
    a, b = own[...], other[...]
    left = jnp.where(first, a, b)
    corner = jnp.where(first, b, a)[HALF:, :]
    inv_first = inverse_factor(left[0:HALF, :])
    below = left[HALF:, :]
    low = dot_nt(below, inv_first)
    inv_last = inverse_factor(corner - dot_nt(low, low))
    inv[0:HALF, 0:HALF] = inv_first
    inv[0:HALF, HALF:] = jnp.zeros((HALF, HALF), F32)
    inv[HALF:, 0:HALF] = -dot_nn(inv_last, dot_nn(low, inv_first))
    inv[HALF:, HALF:] = inv_last


def call(kernel, shapes, scalars, arrays, scratch=(), before=()):
    smem = pl.BlockSpec(memory_space=pltpu.SMEM)
    vmem = pl.BlockSpec(memory_space=pltpu.VMEM)
    anywhere = pl.BlockSpec(memory_space=pl.ANY)
    return pl.pallas_call(
        kernel,
        out_shape=[jax.ShapeDtypeStruct(shape, F32) for shape in shapes],
        in_specs=[smem] * len(scalars) + [vmem] * len(arrays) + [anywhere] * len(before),
        out_specs=[vmem] * len(shapes),
        scratch_shapes=[pltpu.VMEM(shape, F32) for shape in scratch],
        compiler_params=pltpu.CompilerParams(vmem_limit_bytes=VMEM_LIMIT),
        cost_estimate=pl.CostEstimate(flops=1000000, bytes_accessed=100000, transcendentals=0),
    )(*scalars, *arrays, *before)


def ring(size, shift):
    return [(i, (i + shift) % size) for i in range(size)]


def send(value, axis, shift):
    size = {"y": NY, "z": NZ, "col": NX, "rep": 2}[axis]
    return lax.ppermute(value, axis, ring(size, shift))


def shards(tiles, block_row, block_col, live_rows, omega):
    local_tiles = tiles[0, 0]
    slots = jnp.concatenate([block_row[0], block_col[0], live_rows[0]], axis=0)
    pos = jnp.stack([lax.axis_index(a) for a in ("y", "z", "col", "rep")]).astype(jnp.int32)
    big = CB_DEV // NY * BS
    grams = (2 * HALF, HALF)
    chunks = (NZ, 2 * HALF // NZ, HALF)

    def sum_ring(value, axis, before=pos):
        got = [value] + [send(value, axis, k) for k in range(1, 4)]
        return call(sum_kernel, [value.shape], [], got, (), [before])[0]

    def exchange_z(parts):
        return lax.all_to_all(parts, "z", 0, 0)

    def spread_y(line, done):
        before, after = send(line, "y", 1), send(line, "y", NY - 1)
        first, last = call(cut_kernel, [(big // 2, HALF)] * 2, [], [before, after], (), [done])
        return [line, before, after, send(first, "y", 1), send(last, "y", NY - 1)]

    def gather_first(own):
        up, down, far = (send(own, "z", k) for k in (1, NZ - 1, 4))
        low, high = call(pair_kernel, [(2 * COLS_OWN, HALF)] * 2, [], [up, own, down])
        line = [far, send(low, "z", 2), up, own, down, send(high, "z", NZ - 2)]
        return spread_y(call(join_kernel, [(big, HALF)], [], line, (), [pos])[0], pos)

    def gather_panel(own, gram):
        up, down, far = (send(own, "z", k) for k in (1, NZ - 1, 4))
        parts = exchange_z(gram.reshape(chunks))
        part = call(sum_parts_kernel, [chunks[1:]], [], [parts])[0]
        low, high = call(
            fan_kernel, [(2 * COLS_OWN, HALF)] * 2, [], [up, own, down], (), [part]
        )
        line = [far, send(low, "z", 2), up, own, down, send(high, "z", NZ - 2)]
        part = sum_ring(part, "y")
        parts = [part] + [send(part, "col", k) for k in range(1, NX)]
        line = call(join_kernel, [(big, HALF)], [], line, (), [part])[0]
        copies = call(copies_kernel, [chunks], [], parts)[0]
        whole = exchange_z(copies).reshape(grams)
        return spread_y(line, whole), whole

    def gather_rows(own):
        return [own] + [send(own, "col", k) for k in range(1, NX)]

    def forward(pieces, carried):
        *out, passed = call(
            forward_kernel,
            [(ROWS_OWN, HALF)] * NX + [carried.shape],
            [pos, slots],
            [local_tiles, *pieces, carried],
            [(CB_DEV * BS, HALF), (RB_DEV * BS, HALF)],
        )
        return [out[0]] + [send(out[k], "col", k) for k in range(1, NX)], passed

    def forward_sum(got, before):
        return call(sum_kernel, [(ROWS_OWN, HALF)], [], got, (), [before])[0]

    def backward(pieces, gram):
        part = sum_ring(jnp.sum(exchange_z(gram.reshape(chunks)), axis=0), "col")
        far = (big // 2 + part.shape[0], HALF)
        far_part = send(part, "y", 2)
        own, near, far_a, far_b, back = call(
            backward_kernel,
            [(big, HALF)] * 2 + [far] * 2 + [(big, HALF)],
            [pos, slots],
            [local_tiles, *pieces, part],
            [(RB_DEV * BS, HALF), (CB_DEV * BS, HALF)],
        )
        far_a, far_b = send(far_a, "y", 1), send(far_b, "y", NY - 1)
        near, back, copies = call(
            relay_y_kernel,
            [(big, HALF)] * 2 + [chunks],
            [],
            [near, far_a, back, far_b, part, far_part],
        )
        before, after = send(near, "y", 1), send(back, "y", NY - 1)
        mine = exchange_z(copies).reshape(grams)
        piece = (COLS_OWN, HALF)
        up, down, own, near, back, mine = call(
            split_z_kernel,
            [(3 * COLS_OWN, HALF), (2 * COLS_OWN, HALF), piece, piece, piece, grams],
            [pos],
            [own, before, after, mine],
        )
        up, down = send(up, "z", 3), send(down, "z", NZ - 3)
        inv = factor(mine, send(mine, "rep", 1))
        own, near, back = call(
            relay_z_kernel, [piece] * 3, [], [own, near, back, up, down], (), [inv]
        )
        got = [own, send(near, "z", 1), send(back, "z", NZ - 1)]
        return call(sum_three_kernel, [piece], [], got)[0], inv

    def sum_gram(gram):
        count, chunk = NY * NX, 2 * HALF // (NY * NX)
        parts = lax.all_to_all(gram.reshape(count, chunk, HALF), ("y", "col"), 0, 0)
        part = jnp.sum(parts, axis=0)
        parts = lax.all_to_all(jnp.broadcast_to(part[None], (NZ, chunk, HALF)), "z", 0, 0)
        part = jnp.sum(parts, axis=0)
        whole = lax.all_to_all(
            jnp.broadcast_to(part[None], (count, chunk, HALF)), ("y", "col"), 0, 0
        )
        return whole.reshape(grams)

    def factor(mine, other):
        return call(factor_kernel, [(2 * HALF, 2 * HALF)], [pos], [mine, other])[0]

    def normalised(value, inv):
        other = send(value, "rep", 1)
        shape = value.shape
        return call(apply_gram_kernel, [shape, shape, grams], [pos], [value, other, inv])

    def finished(value, other, inv, scale):
        return call(make_apply_scaled(scale), [value.shape], [pos], [value, other, inv])[0]

    got, _ = forward(gather_first(omega[0]), omega[0, 0:8])
    own = forward_sum(got, pos)
    gram = call(gram_kernel, [grams], [pos], [own, send(own, "rep", 1)])[0]
    total_rows = ROWS_OWN * NX * NY * NZ
    total_cols = COLS_OWN * NX * NY * NZ
    for step in range(ITERS):
        value, inv = backward(gather_rows(own), gram)
        panel, panel_other, gram = normalised(value, inv)
        pieces, mine = gather_panel(panel, gram)
        got, other = forward(pieces, send(mine, "rep", 1))
        inv = factor(mine, other)
        if step == ITERS - 1:
            panel_basis = finished(panel, panel_other, inv, math.sqrt(total_cols))
        own, other, gram = normalised(
            forward_sum(got, panel_basis if step == ITERS - 1 else inv), inv
        )
    mine = sum_gram(gram)
    inv = factor(mine, send(mine, "rep", 1))
    basis = finished(own, other, inv, math.sqrt(total_rows))
    return basis[None], panel_basis[None]


def solution(mesh):
    fine = Mesh(mesh.devices.reshape(NY, NZ, NX, 2), ("y", "z", "col", "rep"))
    row = ("y", "z")
    placed = (
        P(row, "col", None, None, None),
        P(row, "col", None),
        P(row, "col", None),
        P(row, "col", None),
        P("col", row, "rep"),
    )
    return jax.shard_map(
        shards,
        mesh=fine,
        in_specs=placed,
        out_specs=(P(row, "col", "rep"), P("col", row, "rep")),
        check_vma=False,
    )
```
